128 devices in a mesh: gx: 8 (over z_lo, y), gy: 16 (over x, z_hi, core).
Axes of the slice: x: 4, y: 4, z: 4 (z_hi: 2, z_lo: 2; z = z_hi * 2 + z_lo), core: 2. Of those that a mesh axis runs over, the one named last changes fastest.
Arguments:
- velocity_now: float32 [3, 64, 256, 512], P(None, 'gx', 'gy'), may hold values from -6 to 6
- advecting: float32 [3, 64, 256, 512], P(None, 'gx', 'gy'), may hold values from -6 to 6
- cotangent: float32 [3, 64, 256, 512], P(None, 'gx', 'gy'), may hold values from -6 to 6
- building_height: int32 [64, 256], P('gx', 'gy'), may hold values from 0 to 127
- section_index: int32 [1], replicated, may hold values from 0 to 191
- vertical_modes: float32 [512, 512], replicated, may hold values from -0.25 to 0.25
- vertical_tilt: float32 [512, 512], replicated, may hold values from -0.25 to 0.25
- mode_rates: float32 [512], replicated, may hold values from 0.01 to 1
Outputs:
- velocity_next: float32 [3, 64, 256, 512], P(None, 'gx', 'gy')
- velocity_adjoint: float32 [3, 64, 256, 512], P(None, 'gx', 'gy')
The draws below stay inside these ranges and needn't reach their ends.
All inputs are finite; a program needn't handle non-finite values.
Results may differ from the reference program's by a relative error of at most 0.000055.
Values sent between devices are 32-bit elements; how exact they have to be, the bound alone decides.
A program may use at most 192 MiB of HBM per device.

```python
import math
import jax
import jax.numpy as jnp
from jax import lax

NZ = 512
NX = 64
NY = 256


def touch_ends(drawn, own_key, smallest, high):
    shape = drawn.shape
    index_at = [jax.random.randint(jax.random.fold_in(own_key, axis), (), 0, shape[axis]) for axis in range(len(shape))]
    drawn = drawn.at[tuple(index_at)].set(smallest)
    longest = shape.index(max(shape))
    index_at[longest] = (index_at[longest] + 1) % shape[longest]
    return drawn.at[tuple(index_at)].set(high)


def block_levels(rng, dims, cuts, least, largest):
    def one(axis_at, blocks):
        heights = jax.random.uniform(jax.random.fold_in(jax.random.fold_in(rng, 6), axis_at), (blocks,), jnp.float32, least / len(cuts), largest / len(cuts))
        return jnp.repeat(jnp.exp(heights), dims[axis_at] // blocks).reshape((-1,) + (1,) * (len(dims) - axis_at - 1))

    gain = one(*cuts[0])
    for cut in cuts[1:]:
        gain = gain * one(*cut)
    return gain


def normal_values(stream_key, shape, width, bound, split=(), kind=jnp.bfloat16):
    entries = jax.random.normal(stream_key, shape, jnp.float32) * width
    if len(split) > 0:
        entries = block_levels(stream_key, shape, split, -0.22, 0.18) * entries
    return jnp.clip(entries, min=-bound, max=bound).astype(kind)


def setup_inputs(seed: int = 0) -> dict:
    key_list = jax.random.split(jax.random.key(seed), 9)
    return {
        "velocity_now": normal_values(key_list[0], (3, NX, NY, NZ), 1.0, 6.0, ((1, 8), (2, 16)), jnp.float32),
        "advecting": normal_values(key_list[1], (3, NX, NY, NZ), 1.0, 6.0, ((1, 8), (2, 16)), jnp.float32),
        "cotangent": normal_values(key_list[2], (3, NX, NY, NZ), 1.0, 6.0, ((1, 8), (2, 16)), jnp.float32),
        "building_height": touch_ends(jax.random.randint(key_list[3], (NX, NY), 0, NZ // 4), jax.random.fold_in(key_list[3], 1), 0, (NZ // 4) - 1).astype(jnp.int32),
        "section_index": jax.random.randint(key_list[4], (1,), 0, 192).astype(jnp.int32),
        "vertical_modes": normal_values(key_list[5], (NZ, NZ), NZ ** -0.5, 0.25, (), jnp.float32),
        "vertical_tilt": normal_values(key_list[6], (NZ, NZ), NZ ** -0.5, 0.25, (), jnp.float32),
        "mode_rates": jnp.clip(jnp.exp(jax.random.uniform(key_list[7], (NZ,), jnp.float32, math.log(0.01), math.log(1.0))), 0.01, 1.0),
    }


stencil_taps = ((2, -1.0, 1.0), (1, 8.0, -4.0), (0, 0.0, 6.0), (-1, -8.0, -4.0), (-2, 1.0, 1.0))
highest = lax.Precision.HIGHEST

def section_factor(section_index):
    section = section_index[0] % 3
    step_number = section_index[0] // 3
    step_size = jnp.float32(0.2) + jnp.float32(0.2) * step_number.astype(jnp.float32) / jnp.float32(63.0)
    fraction = jnp.where(section == 0, jnp.float32(1.0 / 3.0), jnp.where(section == 1, jnp.float32(0.5), jnp.float32(1.0)))
    return step_size * fraction

def upwind(viewer, advect_speed):
    central = 0.0
    hyper_sum = 0.0
    for offset, central_weight, hyper_weight in stencil_taps:
        sample = viewer(offset)
        central = central + central_weight * sample
        hyper_sum = hyper_sum + hyper_weight * sample
    return advect_speed * central + jnp.abs(advect_speed) * hyper_sum

def tendency(velocity, advecting):
    levels = velocity.shape[3]
    column = jnp.pad(velocity, ((0, 0), (0, 0), (0, 0), (2, 2)))

    def view_x(offset):
        return jnp.roll(velocity, -offset, axis=1)

    def view_y(offset):
        return jnp.roll(velocity, -offset, axis=2)

    def view_z(offset):
        return lax.slice_in_dim(column, 2 + offset, 2 + offset + levels, axis=3)
    summed = upwind(view_x, advecting[0][None])
    summed = summed + upwind(view_y, advecting[1][None])
    summed = summed + upwind(view_z, advecting[2][None])
    return -summed / 12.0

def project(fields, vertical_modes, vertical_tilt, mode_rates):
    matrices = jnp.stack([vertical_modes, vertical_modes, vertical_tilt])
    modal_data = jnp.einsum('cxyz,czm->cmxy', fields, matrices, precision=highest)
    spectra = jnp.fft.fft2(modal_data, axes=(2, 3))
    angle_x = jnp.arange(NX, dtype=jnp.int32).astype(jnp.float32) * (2.0 * math.pi / NX)
    angle_y = jnp.arange(NY, dtype=jnp.int32).astype(jnp.float32) * (2.0 * math.pi / NY)
    diff_x = (1.0 - jnp.cos(angle_x) + 1j * jnp.sin(angle_x))[:, None]
    diff_y = (1.0 - jnp.cos(angle_y) + 1j * jnp.sin(angle_y))[None, :]
    lam_sum = jnp.abs(diff_x) ** 2 + jnp.abs(diff_y) ** 2
    divergence = diff_x * spectra[0] + diff_y * spectra[1] + spectra[2]
    potential = divergence / (mode_rates[:, None, None] + lam_sum)
    psi_all = jnp.stack([jnp.conj(diff_x) * potential, jnp.conj(diff_y) * potential, potential])
    physical = jnp.real(jnp.fft.ifft2(psi_all, axes=(2, 3)))
    correction = jnp.einsum('cmxy,czm->cxyz', physical, matrices, precision=highest)
    return fields - correction

def reference(velocity_now, advecting, cotangent, building_height, section_index, vertical_modes, vertical_tilt, mode_rates):
    level_index = lax.broadcasted_iota(jnp.int32, (NX, NY, NZ), 2)
    fluid_cells = (level_index >= building_height[:, :, None]).astype(jnp.float32)
    factor = section_factor(section_index)
    section_value = fluid_cells * (velocity_now + factor * tendency(velocity_now, advecting))
    velocity_next = project(section_value, vertical_modes, vertical_tilt, mode_rates)
    gradient = fluid_cells * project(cotangent, vertical_modes, vertical_tilt, mode_rates)
    pullback_fn = jax.vjp(lambda field: tendency(field, advecting), gradient)[1]
    pullback = pullback_fn(gradient)[0]
    velocity_adjoint = gradient + factor * pullback
    return (velocity_next, velocity_adjoint)
```

```python
import functools
import math

import jax
import jax.numpy as jnp
import ml_dtypes
import numpy as np
from jax import lax
from jax.experimental import pallas as pl
from jax.experimental.pallas import tpu as pltpu
from jax.sharding import PartitionSpec as P

MESH = pl.DeviceIdType.MESH
BX, BY = 8, 16
GX, GY = 8, 16
NX, NY, NZ = 64, 256, 512
DEVICES = GX * GY
OWNED = NZ // DEVICES
SLOTS = 64
f32, bf16 = jnp.float32, jnp.bfloat16


def fourier(n):
    place = np.arange(n)
    basis = np.zeros((n, n))
    freq = np.zeros(n)
    for column in range(n):
        k = (column + 1) // 2
        angle = 2.0 * math.pi * k * place / n
        if column == 0 or k == n // 2:
            basis[:, column] = np.cos(angle) / math.sqrt(n)
        else:
            basis[:, column] = (np.cos(angle) if column % 2 else np.sin(angle)) * math.sqrt(2.0 / n)
        freq[column] = 2.0 - 2.0 * math.cos(2.0 * math.pi * k / n)
    return basis, freq


def split_const(matrix):
    high = matrix.astype(ml_dtypes.bfloat16)
    low = (matrix - high.astype(np.float64)).astype(ml_dtypes.bfloat16)
    return high, low


def tables():
    j, k = np.arange(BX), np.arange(BY)
    sin_x = math.sqrt(2.0 / BX) * np.sin(math.pi * np.outer(j, j) / BX)
    sin_y = math.sqrt(2.0 / BY) * np.sin(math.pi * np.outer(k, k) / BY)
    sin_x[0], sin_x[:, 0], sin_y[0], sin_y[:, 0] = 0.0, 0.0, 0.0, 0.0
    sine = np.kron(sin_x, sin_y)
    mu = (2.0 - 2.0 * np.cos(math.pi * j / BX))[:, None] + (2.0 - 2.0 * np.cos(math.pi * k / BY))
    mu = np.repeat(mu.reshape(-1, 1), 128, axis=1)
    near = np.zeros((SLOTS, BX * BY))
    own = np.zeros((SLOTS, BX * BY))
    for y in range(BY):
        own[y, y] = 1.0
        if y:
            near[y] = sine[1 * BY + y]
            near[16 + y] = sine[(BX - 1) * BY + y]
    for x in range(1, BX):
        own[32 + x, x * BY] = 1.0
        near[32 + x] = sine[x * BY + 1]
        near[40 + x] = sine[x * BY + BY - 1]
    to_slots = np.concatenate([near, own], 1)
    from_slots = np.concatenate([sine, own.T], 1)
    qx, lx = fourier(NX)
    qy, ly = fourier(NY)
    w1 = np.zeros((GY, SLOTS, 3, 256))
    for g in range(GY):
        w1[g, 0:16, 0] = qy[16 * g : 16 * g + 16]
        w1[g, 16:32, 1] = qy[16 * g : 16 * g + 16]
        for x in range(BX):
            for kind in range(2):
                w1[g, 32 + 8 * kind + x, 2, x * 32 + kind * 16 + g] = 1.0
    w1 = w1.reshape(GY * SLOTS, 768)
    rows = np.zeros((2, NX, OWNED, 2, 2, GX, OWNED))
    cols = np.zeros((2, NX, OWNED, BX, 2, GX, OWNED))
    for group in range(2):
        for mode in range(OWNED):
            for g in range(GX):
                for kind in range(2):
                    rows[group, :, mode, kind, group, g, mode] = qx[8 * (g + kind) % NX]
                for x in range(BX):
                    cols[group, :, mode, x, group, g, mode] = qx[8 * g + x]
    rows = rows.reshape(512, 128)
    cols = cols.reshape(512, 512)
    wc = np.stack([qy[0::16], np.roll(qy[0::16], -1, axis=0)]).reshape(32, 256)
    lam_x = np.repeat(np.broadcast_to(lx[None, :, None], (2, NX, OWNED)).reshape(512, 1), 128, axis=1)
    lam_y = ly[None, :]
    split = [sine, to_slots, near.T, from_slots, w1, rows, rows.T, cols, cols.T, wc, wc.T]
    out = []
    for matrix in split:
        out.extend(split_const(np.ascontiguousarray(matrix)))
    plain = [mu.astype(np.float32), lam_x.astype(np.float32), lam_y.astype(np.float32)]
    return [jnp.asarray(t) for t in out + plain]


def halves(value):
    high = value.astype(bf16)
    low = (value - high.astype(f32)).astype(bf16)
    return high, low


def dot(a, b, nt=False):
    dims = (((1,), (1 if nt else 0,)), ((), ()))
    return lax.dot_general(a, b, dims, preferred_element_type=f32)


def dot3(a, b, nt=False):
    return dot(a[0], b[0], nt) + (dot(a[0], b[1], nt) + dot(a[1], b[0], nt))


def wide(column, lanes):
    return jnp.concatenate([column] * (lanes // 128), axis=1)


TAPS = ((-2, 1.0, 1.0), (-1, -8.0, -4.0), (0, 0.0, 6.0), (1, 8.0, -4.0), (2, -1.0, 1.0))


def weights(speed):
    size = jnp.abs(speed)
    out = {}
    for offset, central, hyper in TAPS:
        out[offset] = hyper * size + central * speed if central else hyper * size
    return out


def moved(value, offset, axis):
    n = value.shape[axis]
    if axis == 1:
        rolled = pltpu.roll(value, (-offset) % n, 1)
    else:
        rolled = jnp.roll(value, -offset, 0)
    place = lax.broadcasted_iota(jnp.int32, value.shape, axis)
    keep = place < n - offset if offset > 0 else place >= -offset
    return jnp.where(keep, rolled, 0.0)


def kernel(
    vel, adv, cot, height, section, vm_ref, vt_ref, rate_row, rate_s,
    sine_h, sine_l, ts_h, ts_l, nt_h, nt_l, fs_h, fs_l, w1_h, w1_l, rw_h, rw_l, rt_h, rt_l,
    cl_h, cl_l, ct_h, ct_l, wc_h, wc_l, wt_h, wt_l, mu_ref, lamx_ref, lamy_ref,
    next_ref, adj_ref,
    vb, sv, lhs, vh, vl, th, tl, ys, yr, sb, rbuf, ob, rb, xs, cx, gp, sxp, cxs, cxr, cys, cyr,
    d_ref, p1_ref, ie_ref,
    a_send, a_recv, h_send, h_recv, l_sem,
):
    gx, gy = lax.axis_index("gx"), lax.axis_index("gy")
    me = gx * GY + gy
    left_x, right_x = lax.rem(gx + GX - 1, GX), lax.rem(gx + 1, GX)
    left_y, right_y = lax.rem(gy + GY - 1, GY), lax.rem(gy + 1, GY)

    def other(i):
        t = lax.rem(me + i, DEVICES)
        return t, lax.div(t, GY), lax.rem(t, GY)

    barrier = pltpu.get_barrier_semaphore()

    def greet(i, carry):
        _, tx, ty = other(i)
        pl.semaphore_signal(barrier, inc=1, device_id=(tx, ty), device_id_type=MESH)
        return carry

    lax.fori_loop(1, DEVICES, greet, 0)

    for c in range(3):
        for x in range(BX):
            ys[0, c, 2 * x : 2 * x + 2, :] = vel[c, x, 0:2, :]
            ys[1, c, 2 * x : 2 * x + 2, :] = vel[c, x, BY - 2 : BY, :]

    pl.semaphore_wait(barrier, DEVICES - 1)

    def remote(src, dst, n, x, y):
        return pltpu.make_async_remote_copy(
            src_ref=src, dst_ref=dst, send_sem=h_send.at[n], recv_sem=h_recv.at[n],
            device_id=(x, y), device_id_type=MESH,
        )

    halo = [
        remote(vel.at[:, pl.ds(0, 2)], vb.at[:, pl.ds(BX + 2, 2), pl.ds(8, BY)], 0, left_x, gy),
        remote(vel.at[:, pl.ds(BX - 2, 2)], vb.at[:, pl.ds(0, 2), pl.ds(8, BY)], 1, right_x, gy),
        remote(ys.at[0], yr.at[1], 2, gx, left_y),
        remote(ys.at[1], yr.at[0], 3, gx, right_y),
    ]
    for copy in halo:
        copy.start()

    for c in range(3):
        vb[c, 2 : BX + 2, 8 : 8 + BY, :] = vel[c]
    for full, high, low in ((vm_ref, vh, vl), (vt_ref, th, tl)):
        for i in range(0, NZ, 64):
            h, l = halves(full[i : i + 64, :])
            high[i : i + 64, :] = h
            low[i : i + 64, :] = l
    ie_ref[...] = 1.0 / (wide(mu_ref[...], NZ) + rate_row[...])

    number = section[0]
    part = lax.rem(number, 3)
    step = lax.div(number, 3).astype(f32)
    fraction = jnp.where(part == 0, f32(1.0 / 3.0), jnp.where(part == 1, f32(0.5), f32(1.0)))
    factor = (f32(0.2) + step * f32(0.2 / 63.0)) * fraction
    scale = factor * f32(-1.0 / 12.0)

    levels = lax.broadcasted_iota(jnp.int32, (BY, NZ), 1).astype(f32)
    diagonal = lax.broadcasted_iota(jnp.int32, (BY, BY), 0) == lax.broadcasted_iota(
        jnp.int32, (BY, BY), 1
    )

    def fluid_at(x):
        row = height[pl.ds(x, 1), :].astype(f32)
        column = jnp.sum(jnp.where(diagonal, row, 0.0), axis=1, keepdims=True)
        return (levels >= column).astype(f32)

    def left_sides(group, field):
        for x in range(BX):
            f0 = field[0, x]
            if x:
                f0 = f0 - field[0, x - 1]
            f1 = field[1, x]
            lhs[group, BY * x : BY * x + BY, :] = f0 + (f1 - moved(f1, -1, 0))
            lhs[group, 144 + x : 145 + x, :] = -field[1, x, BY - 1 : BY, :]
        lhs[group, 128:144, :] = -field[0, BX - 1]
        lhs[group, 152:160, :] = jnp.zeros((8, NZ), f32)

    def forward(group, field):
        left_sides(group, field)
        wide_rows = dot3(halves(lhs[group]), (vh[...], vl[...]))
        tilted = dot3(halves(field[2].reshape(BX * BY, NZ)), (th[...], tl[...]))
        d = wide_rows[:128] + tilted
        d_parts = halves(d)
        p1 = dot3((sine_h[...], sine_l[...]), d_parts)
        p1_ref[group] = p1
        w = halves(p1 * ie_ref[...])
        both = (
            jnp.concatenate([w[0], d_parts[0]], axis=0),
            jnp.concatenate([w[1], d_parts[1]], axis=0),
        )
        s = dot3((ts_h[...], ts_l[...]), both)
        d_ref[group * SLOTS : group * SLOTS + 64, :] = s
        d_ref[group * SLOTS + 16 : group * SLOTS + 32, :] += wide_rows[128:144]
        d_ref[group * SLOTS + 40 : group * SLOTS + 48, :] += wide_rows[144:152]

    forward(1, cot)

    for copy in halo:
        copy.wait()
    for c in range(3):
        for x in range(BX):
            vb[c, x + 2, 6:8, :] = yr[0, c, 2 * x : 2 * x + 2, :]
            vb[c, x + 2, 8 + BY : 10 + BY, :] = yr[1, c, 2 * x : 2 * x + 2, :]

    def section_row(x, carry):
        fluid = fluid_at(x)
        kx, ky, kz = weights(adv[0, x]), weights(adv[1, x]), weights(adv[2, x])
        for c in range(3):
            center = vb[c, x + 2, 8 : 8 + BY, :]
            total = center * (kx[0] + ky[0] + kz[0])
            for offset in (-2, -1, 1, 2):
                total = total + kx[offset] * vb[c, x + 2 + offset, 8 : 8 + BY, :]
                total = total + ky[offset] * vb[c, x + 2, 8 + offset : 8 + BY + offset, :]
                total = total + kz[offset] * moved(center, offset, 1)
            sv[c, x] = fluid * (center + scale * total)
        return carry

    lax.fori_loop(0, BX, section_row, 0)
    forward(0, sv)

    for i in range(4):
        sb[128 * i : 128 * i + 128, :] = d_ref[:, 128 * i : 128 * i + 128].T

    def exchange(n, src, dst, src_row, dst_row):
        def start(i, carry):
            t, tx, ty = other(i)
            pltpu.make_async_remote_copy(
                src_ref=src.at[pl.ds(src_row(t, tx, ty) * OWNED, OWNED)],
                dst_ref=dst.at[pl.ds(dst_row * OWNED, OWNED)],
                send_sem=a_send.at[n], recv_sem=a_recv.at[n],
                device_id=(tx, ty), device_id_type=MESH,
            ).start()
            return carry

        lax.fori_loop(1, DEVICES, start, 0)
        local = pltpu.make_async_copy(
            src.at[pl.ds(src_row(me, gx, gy) * OWNED, OWNED)],
            dst.at[pl.ds(dst_row * OWNED, OWNED)],
            l_sem.at[n],
        )
        local.start()
        local.wait()
        whole = pltpu.make_async_remote_copy(
            src_ref=src.at[pl.ds(0, (DEVICES - 1) * OWNED)],
            dst_ref=dst.at[pl.ds(0, (DEVICES - 1) * OWNED)],
            send_sem=a_send.at[n], recv_sem=a_recv.at[n],
            device_id=(right_x, gy), device_id_type=MESH,
        )
        whole.wait_send()
        whole.wait_recv()

    place = gy * GX + gx
    exchange(0, sb, rbuf, lambda t, tx, ty: t, place)

    low_lanes = lax.broadcasted_iota(jnp.int32, (32, 128), 1) < SLOTS
    for pair in range(GY // 2):
        a = rbuf[64 * pair : 64 * pair + 32, :]
        b = rbuf[64 * pair + 32 : 64 * pair + 64, :]
        xs[0:32, 128 * pair : 128 * pair + 128] = jnp.where(low_lanes, a, pltpu.roll(b, 64, 1))
        xs[32:64, 128 * pair : 128 * pair + 128] = jnp.where(low_lanes, pltpu.roll(a, 64, 1), b)
    y1 = dot3(halves(xs[...]), (w1_h[...], w1_l[...]))
    stacked = jnp.concatenate([y1[:, 0:256], y1[:, 256:512]], axis=0)
    for x in range(BX):
        cx[64 * x : 64 * x + 64, :] = y1[:, 512 + 32 * x : 544 + 32 * x]
    hat = dot3((rw_h[...], rw_l[...]), halves(stacked))
    inner = dot3((cl_h[...], cl_l[...]), halves(cx[...]))
    hat = hat + dot3(halves(inner), (wc_h[...], wc_l[...]))
    row_mode = lax.rem(lax.broadcasted_iota(jnp.int32, (512, 128), 0), OWNED)
    rate = jnp.zeros((512, 128), f32)
    for m in range(OWNED):
        rate = jnp.where(row_mode == m, rate_s[me * OWNED + m], rate)
    hat = hat / (wide(rate + lamx_ref[...], 256) + lamy_ref[...])
    hat_parts = halves(hat)
    back = dot3((rt_h[...], rt_l[...]), hat_parts)
    inner = dot3(hat_parts, (wt_h[...], wt_l[...]))
    cx[...] = dot3((ct_h[...], ct_l[...]), halves(inner))
    parts = [back[0:64], back[64:128]] + [cx[64 * x : 64 * x + 64, :] for x in range(BX)]
    xs[...] = dot3(halves(jnp.concatenate(parts, axis=1)), (w1_h[...], w1_l[...]), nt=True)
    for pair in range(GY // 2):
        p = xs[0:32, 128 * pair : 128 * pair + 128]
        q = xs[32:64, 128 * pair : 128 * pair + 128]
        ob[64 * pair : 64 * pair + 32, :] = jnp.where(low_lanes, p, pltpu.roll(q, 64, 1))
        ob[64 * pair + 32 : 64 * pair + 64, :] = jnp.where(low_lanes, pltpu.roll(p, 64, 1), q)

    exchange(1, ob, rb, lambda t, tx, ty: ty * GX + tx, me)

    for i in range(4):
        d_ref[:, 128 * i : 128 * i + 128] = rb[128 * i : 128 * i + 128, :].T

    def backward(group):
        u = d_ref[group * SLOTS : group * SLOTS + SLOTS, :]
        u_parts = halves(u)
        inside = (p1_ref[group] + dot3((nt_h[...], nt_l[...]), u_parts)) * ie_ref[...]
        in_parts = halves(inside)
        both = (
            jnp.concatenate([in_parts[0], u_parts[0]], axis=0),
            jnp.concatenate([in_parts[1], u_parts[1]], axis=0),
        )
        phi = dot3((fs_h[...], fs_l[...]), both)
        ext = jnp.concatenate([phi, u[16:32], u[40:48], jnp.zeros((8, NZ), f32)], axis=0)
        lhs[group] = dot3(halves(ext), (vh[...], vl[...]), nt=True)
        return dot3(halves(phi), (th[...], tl[...]), nt=True)

    def corrections(group, x):
        here = lhs[group, BY * x : BY * x + BY, :]
        after = lhs[group, BY * x + BY : BY * x + 2 * BY, :]
        last = lax.broadcasted_iota(jnp.int32, (BY, NZ), 0) == BY - 1
        side = jnp.where(last, lhs[group, 144 + x : 145 + x, :], jnp.roll(here, -1, 0))
        return here - after, here - side

    tilted = backward(1)
    for x in range(BX):
        fluid = fluid_at(x)
        c0, c1 = corrections(1, x)
        gp[0, x + 2] = fluid * (cot[0, x] - c0)
        gp[1, x + 2] = fluid * (cot[1, x] - c1)
        gp[2, x + 2] = fluid * (cot[2, x] - tilted[BY * x : BY * x + BY])
        sxp[x + 2] = adv[0, x]
    nothing = jnp.zeros((2, BY, NZ), f32)
    for c in range(3):
        gp[c, 0:2] = nothing
        gp[c, BX + 2 : BX + 4] = nothing
    sxp[0:2] = nothing
    sxp[BX + 2 : BX + 4] = nothing

    k0, k1 = weights(adv[0, 0]), weights(adv[0, 1])
    k6, k7 = weights(adv[0, BX - 2]), weights(adv[0, BX - 1])
    for c in range(3):
        g0, g1, g6, g7 = gp[c, 2], gp[c, 3], gp[c, BX], gp[c, BX + 1]
        cxs[0, c, 0] = k0[-2] * g0
        cxs[0, c, 1] = k0[-1] * g0 + k1[-2] * g1
        cxs[1, c, 0] = k7[1] * g7 + k6[2] * g6
        cxs[1, c, 1] = k7[2] * g7
    for x in range(BX):
        k = weights(adv[1, x])
        for c in range(3):
            g = gp[c, x + 2]
            one, two = k[-1] * g, k[-2] * g
            cys[0, c, 2 * x : 2 * x + 1, :] = two[0:1]
            cys[0, c, 2 * x + 1 : 2 * x + 2, :] = one[0:1] + two[1:2]
            one, two = k[1] * g, k[2] * g
            cys[1, c, 2 * x : 2 * x + 1, :] = one[BY - 1 : BY] + two[BY - 2 : BY - 1]
            cys[1, c, 2 * x + 1 : 2 * x + 2, :] = two[BY - 1 : BY]
    edges = [
        remote(cxs.at[0], cxr.at[1], 4, left_x, gy),
        remote(cxs.at[1], cxr.at[0], 5, right_x, gy),
        remote(cys.at[0], cyr.at[1], 6, gx, left_y),
        remote(cys.at[1], cyr.at[0], 7, gx, right_y),
    ]
    for copy in edges:
        copy.start()

    tilted = backward(0)
    for x in range(BX):
        c0, c1 = corrections(0, x)
        next_ref[0, x] = sv[0, x] - c0
        next_ref[1, x] = sv[1, x] - c1
        next_ref[2, x] = sv[2, x] - tilted[BY * x : BY * x + BY]

    def adjoint_row(x, carry):
        kx = {}
        for offset in (-2, -1, 0, 1, 2):
            kx[offset] = weights(sxp[x + 2 - offset])[offset]
        ky, kz = weights(adv[1, x]), weights(adv[2, x])
        for c in range(3):
            center = gp[c, x + 2]
            total = center * (kx[0] + ky[0] + kz[0])
            for offset in (-2, -1, 1, 2):
                total = total + kx[offset] * gp[c, x + 2 - offset]
                total = total + moved(ky[offset] * center, -offset, 0)
                total = total + moved(kz[offset] * center, -offset, 1)
            adj_ref[c, x] = center + scale * total
        return carry

    lax.fori_loop(0, BX, adjoint_row, 0)
    for copy in edges:
        copy.wait()
    for c in range(3):
        for n in range(2):
            adj_ref[c, n] += scale * cxr[0, c, n]
            adj_ref[c, BX - 2 + n] += scale * cxr[1, c, n]
        for x in range(BX):
            adj_ref[c, x, 0:2, :] += scale * cyr[0, c, 2 * x : 2 * x + 2, :]
            adj_ref[c, x, BY - 2 : BY, :] += scale * cyr[1, c, 2 * x : 2 * x + 2, :]


def per_device(
    velocity_now, advecting, cotangent, building_height, section_index,
    vertical_modes, vertical_tilt, mode_rates,
):
    constants = tables()
    vmem = pl.BlockSpec(memory_space=pltpu.VMEM)
    smem = pl.BlockSpec(memory_space=pltpu.SMEM)
    field = jax.ShapeDtypeStruct((3, BX, BY, NZ), f32)
    return pl.pallas_call(
        kernel,
        out_shape=(field, field),
        in_specs=[vmem, vmem, vmem, vmem, smem, vmem, vmem, vmem, smem] + [vmem] * len(constants),
        out_specs=(vmem, vmem),
        scratch_shapes=[
            pltpu.VMEM((3, BX + 4, 32, NZ), f32),
            pltpu.VMEM((3, BX, BY, NZ), f32),
            pltpu.VMEM((2, 160, NZ), f32),
            pltpu.VMEM((NZ, NZ), bf16),
            pltpu.VMEM((NZ, NZ), bf16),
            pltpu.VMEM((NZ, NZ), bf16),
            pltpu.VMEM((NZ, NZ), bf16),
            pltpu.VMEM((2, 3, 16, NZ), f32),
            pltpu.VMEM((2, 3, 16, NZ), f32),
            pltpu.VMEM((NZ, 128), f32),
            pltpu.VMEM((NZ, 128), f32),
            pltpu.VMEM((NZ, 128), f32),
            pltpu.VMEM((NZ, 128), f32),
            pltpu.VMEM((64, 1024), f32),
            pltpu.VMEM((512, 32), f32),
            pltpu.VMEM((3, BX + 4, BY, NZ), f32),
            pltpu.VMEM((BX + 4, BY, NZ), f32),
            pltpu.VMEM((2, 3, 2, BY, NZ), f32),
            pltpu.VMEM((2, 3, 2, BY, NZ), f32),
            pltpu.VMEM((2, 3, 16, NZ), f32),
            pltpu.VMEM((2, 3, 16, NZ), f32),
            pltpu.VMEM((128, NZ), f32),
            pltpu.VMEM((2, 128, NZ), f32),
            pltpu.VMEM((128, NZ), f32),
            pltpu.SemaphoreType.DMA((2,)),
            pltpu.SemaphoreType.DMA((2,)),
            pltpu.SemaphoreType.DMA((8,)),
            pltpu.SemaphoreType.DMA((8,)),
            pltpu.SemaphoreType.DMA((2,)),
        ],
        compiler_params=pltpu.CompilerParams(
            collective_id=0, has_side_effects=True, vmem_limit_bytes=56 * 1024 * 1024
        ),
    )(
        velocity_now, advecting, cotangent, building_height, section_index,
        vertical_modes, vertical_tilt, mode_rates.reshape(1, NZ), mode_rates, *constants,
    )


def solution(mesh):
    blocks = P(None, "gx", "gy", None)
    return jax.shard_map(
        per_device,
        mesh=mesh,
        in_specs=(blocks, blocks, blocks, P("gx", "gy"), P(), P(), P(), P()),
        out_specs=(blocks, blocks),
        check_vma=False,
    )
```

```python
import functools
import math

import jax
import jax.numpy as jnp
import ml_dtypes
import numpy as np
from jax import lax
from jax.experimental import pallas as pl
from jax.experimental.pallas import tpu as pltpu
from jax.sharding import PartitionSpec as P

MESH = pl.DeviceIdType.MESH
BX, BY = 8, 16
GX, GY = 8, 16
NX, NY, NZ = 64, 256, 512
DEVICES = GX * GY
OWNERS = DEVICES // 2
OWNED = NZ // OWNERS // 2
SLOTS = 64
f32, bf16 = jnp.float32, jnp.bfloat16


def fourier(n):
    place = np.arange(n)
    basis = np.zeros((n, n))
    freq = np.zeros(n)
    for column in range(n):
        k = (column + 1) // 2
        angle = 2.0 * math.pi * k * place / n
        if column == 0 or k == n // 2:
            basis[:, column] = np.cos(angle) / math.sqrt(n)
        else:
            basis[:, column] = (np.cos(angle) if column % 2 else np.sin(angle)) * math.sqrt(2.0 / n)
        freq[column] = 2.0 - 2.0 * math.cos(2.0 * math.pi * k / n)
    return basis, freq


def split_const(matrix):
    high = matrix.astype(ml_dtypes.bfloat16)
    low = (matrix - high.astype(np.float64)).astype(ml_dtypes.bfloat16)
    return high, low


def tables():
    j, k = np.arange(BX), np.arange(BY)
    sin_x = math.sqrt(2.0 / BX) * np.sin(math.pi * np.outer(j, j) / BX)
    sin_y = math.sqrt(2.0 / BY) * np.sin(math.pi * np.outer(k, k) / BY)
    sin_x[0], sin_x[:, 0], sin_y[0], sin_y[:, 0] = 0.0, 0.0, 0.0, 0.0
    sine = np.kron(sin_x, sin_y)
    mu = (2.0 - 2.0 * np.cos(math.pi * j / BX))[:, None] + (2.0 - 2.0 * np.cos(math.pi * k / BY))
    mu = np.repeat(mu.reshape(-1, 1), 128, axis=1)
    near = np.zeros((SLOTS, BX * BY))
    own = np.zeros((SLOTS, BX * BY))
    for y in range(BY):
        own[y, y] = 1.0
        if y:
            near[y] = sine[1 * BY + y]
            near[16 + y] = sine[(BX - 1) * BY + y]
    for x in range(1, BX):
        own[32 + x, x * BY] = 1.0
        near[32 + x] = sine[x * BY + 1]
        near[40 + x] = sine[x * BY + BY - 1]
    to_slots = np.concatenate([near, own], 1)
    from_slots = np.concatenate([sine, own.T], 1)
    qx, lx = fourier(NX)
    qy, ly = fourier(NY)
    order = np.zeros((GY, 2, BX, BX, 2, GY))
    for g in range(GY):
        for kind in range(2):
            for x in range(BX):
                order[g, kind, x, x, kind, g] = 1.0
    order = order.reshape(256, 256)
    rows = np.zeros((2, NX, OWNED, 2, 2, GX, OWNED))
    cols = np.zeros((2, NX, OWNED, BX, 2, GX, OWNED))
    for group in range(2):
        for mode in range(OWNED):
            for g in range(GX):
                for kind in range(2):
                    rows[group, :, mode, kind, group, g, mode] = qx[8 * (g + kind) % NX]
                for x in range(BX):
                    cols[group, :, mode, x, group, g, mode] = qx[8 * g + x]
    rows = rows.reshape(512, 128)
    cols = cols.reshape(512, 512)
    wc = np.stack([qy[0::16], np.roll(qy[0::16], -1, axis=0)]).reshape(32, 256)
    lam_x = np.repeat(np.broadcast_to(lx[None, :, None], (2, NX, OWNED)).reshape(512, 1), 128, axis=1)
    lam_y = ly[None, :]
    out = []
    for matrix in [sine, to_slots, near.T, from_slots, qy, qy.T, rows, rows.T, wc, wc.T]:
        out.extend(split_const(np.ascontiguousarray(matrix)))
    for matrix in [order, order.T]:
        out.append(matrix.astype(ml_dtypes.bfloat16))
    large = np.stack(split_const(cols) + split_const(cols.T))
    plain = [mu.astype(np.float32), lam_x.astype(np.float32), lam_y.astype(np.float32)]
    return [jnp.asarray(t) for t in [large] + out + plain]


def halves(value):
    high = value.astype(bf16)
    low = (value - high.astype(f32)).astype(bf16)
    return high, low


def dot(a, b, nt=False):
    dims = (((1,), (1 if nt else 0,)), ((), ()))
    return lax.dot_general(a, b, dims, preferred_element_type=f32)


def dot_narrow(a, b):
    n = b[0].shape[1]
    both = dot(a[0], jnp.concatenate([b[0], b[1]], axis=1))
    return both[:, :n] + (both[:, n:] + dot(a[1], b[0]))


def regroup(blocks):
    blocks = list(blocks)
    group = lax.broadcasted_iota(jnp.int32, blocks[0].shape, 1) // 16
    for step in (4, 2, 1):
        low = (group & step) == 0
        for i in range(8):
            if not i & step:
                a, b = blocks[i], blocks[i + step]
                blocks[i] = jnp.where(low, a, pltpu.roll(b, 16 * step, 1))
                blocks[i + step] = jnp.where(low, pltpu.roll(a, 128 - 16 * step, 1), b)
    return blocks


def dot3(a, b, nt=False):
    return dot(a[0], b[0], nt) + (dot(a[0], b[1], nt) + dot(a[1], b[0], nt))


def wide(column, lanes):
    return jnp.concatenate([column] * (lanes // 128), axis=1)


TAPS = ((-2, 1.0, 1.0), (-1, -8.0, -4.0), (0, 0.0, 6.0), (1, 8.0, -4.0), (2, -1.0, 1.0))


def weights(speed):
    size = jnp.abs(speed)
    out = {}
    for offset, central, hyper in TAPS:
        out[offset] = hyper * size + central * speed if central else hyper * size
    return out


def moved(value, offset, axis):
    n = value.shape[axis]
    if axis == 1:
        rolled = pltpu.roll(value, (-offset) % n, 1)
    else:
        rolled = jnp.roll(value, -offset, 0)
    place = lax.broadcasted_iota(jnp.int32, value.shape, axis)
    keep = place < n - offset if offset > 0 else place >= -offset
    return jnp.where(keep, rolled, 0.0)


def kernel(
    vel_h, adv_h, cot_h, height, section, vm_h, vt_h, rate_row, rate_s, large_h,
    sine_h, sine_l, ts_h, ts_l, nt_h, nt_l, fs_h, fs_l, qy_h, qy_l, qt_h, qt_l, rw_h, rw_l, rt_h, rt_l,
    wc_h, wc_l, wt_h, wt_l, order_ref, ordert_ref, mu_ref, lamx_ref, lamy_ref,
    next_ref, adj_ref,
    vb, adv, cot, vm_ref, vt_ref, large,
    sv, lhs, vh, vl, th, tl, ys, yr, sb, rbuf, ob, rb, gp, sxp, cxs, cxr, cys, cyr,
    p1_ref, ie_ref,
    a_send, a_recv, h_send, h_recv, l_sem, all_sem,
):
    gx, gy = lax.axis_index("gx"), lax.axis_index("gy")
    me = gx * GY + gy
    left_x, right_x = lax.rem(gx + GX - 1, GX), lax.rem(gx + 1, GX)
    left_y, right_y = lax.rem(gy + GY - 1, GY), lax.rem(gy + 1, GY)

    parity, owner = lax.rem(gy, 2), gx * 8 + lax.div(gy, 2)
    barrier = pltpu.get_barrier_semaphore()
    for i in range(1, GX):
        pl.semaphore_signal(barrier, inc=1, device_id=(lax.rem(gx + i, GX), gy), device_id_type=MESH)
    for i in range(1, GY):
        pl.semaphore_signal(barrier, inc=1, device_id=(gx, lax.rem(gy + i, GY)), device_id_type=MESH)

    loads = [
        pltpu.make_async_copy(source, target, l_sem.at[n])
        for n, (source, target) in enumerate(
            (
                (vel_h, vb.at[:, pl.ds(2, BX), pl.ds(8, BY)]),
                (vm_h, vm_ref),
                (vt_h, vt_ref),
                (cot_h, cot),
                (adv_h, adv),
                (large_h, large),
            )
        )
    ]
    for load in loads:
        load.start()
    loads[0].wait()

    for c in range(3):
        for x in range(BX):
            ys[0, c, 2 * x : 2 * x + 2, :] = vb[c, x + 2, 8:10, :]
            ys[1, c, 2 * x : 2 * x + 2, :] = vb[c, x + 2, 6 + BY : 8 + BY, :]

    pl.semaphore_wait(barrier, GX + GY - 2)

    def remote(src, dst, n, x, y):
        return pltpu.make_async_remote_copy(
            src_ref=src, dst_ref=dst, send_sem=h_send.at[n], recv_sem=h_recv.at[n],
            device_id=(x, y), device_id_type=MESH,
        )

    halo = [
        remote(vel_h.at[:, pl.ds(0, 2)], vb.at[:, pl.ds(BX + 2, 2), pl.ds(8, BY)], 0, left_x, gy),
        remote(vel_h.at[:, pl.ds(BX - 2, 2)], vb.at[:, pl.ds(0, 2), pl.ds(8, BY)], 1, right_x, gy),
        remote(ys.at[0], yr.at[1], 2, gx, left_y),
        remote(ys.at[1], yr.at[0], 3, gx, right_y),
    ]
    for copy in halo:
        copy.start()

    for i in range(1, GY):
        pl.semaphore_signal(all_sem, inc=1, device_id=(gx, lax.rem(gy + i, GY)), device_id_type=MESH)

    loads[1].wait()
    loads[2].wait()
    for full, high, low in ((vm_ref, vh, vl), (vt_ref, th, tl)):
        for i in range(0, NZ, 64):
            h, l = halves(full[i : i + 64, :])
            high[i : i + 64, :] = h
            low[i : i + 64, :] = l
    ie_ref[...] = 1.0 / (wide(mu_ref[...], NZ) + rate_row[...])

    number = section[0]
    part = lax.rem(number, 3)
    step = lax.div(number, 3).astype(f32)
    fraction = jnp.where(part == 0, f32(1.0 / 3.0), jnp.where(part == 1, f32(0.5), f32(1.0)))
    factor = (f32(0.2) + step * f32(0.2 / 63.0)) * fraction
    scale = factor * f32(-1.0 / 12.0)

    levels = lax.broadcasted_iota(jnp.int32, (BY, NZ), 1).astype(f32)
    diagonal = lax.broadcasted_iota(jnp.int32, (BY, BY), 0) == lax.broadcasted_iota(
        jnp.int32, (BY, BY), 1
    )

    def fluid_at(x):
        row = height[pl.ds(x, 1), :].astype(f32)
        column = jnp.sum(jnp.where(diagonal, row, 0.0), axis=1, keepdims=True)
        return (levels >= column).astype(f32)

    def left_sides(group, field):
        for x in range(BX):
            f0 = field[0, x]
            if x:
                f0 = f0 - field[0, x - 1]
            f1 = field[1, x]
            lhs[group, BY * x : BY * x + BY, :] = f0 + (f1 - moved(f1, -1, 0))
            lhs[group, 144 + x : 145 + x, :] = -field[1, x, BY - 1 : BY, :]
        lhs[group, 128:144, :] = -field[0, BX - 1]
        lhs[group, 152:160, :] = jnp.zeros((8, NZ), f32)

    def forward(group, field):
        left_sides(group, field)
        wide_rows = dot3(halves(lhs[group]), (vh[...], vl[...]))
        tilted = dot3(halves(field[2].reshape(BX * BY, NZ)), (th[...], tl[...]))
        d = wide_rows[:128] + tilted
        d_parts = halves(d)
        p1 = dot3((sine_h[...], sine_l[...]), d_parts)
        p1_ref[group] = p1
        w = halves(p1 * ie_ref[...])
        both = (
            jnp.concatenate([w[0], d_parts[0]], axis=0),
            jnp.concatenate([w[1], d_parts[1]], axis=0),
        )
        s = dot3((ts_h[...], ts_l[...]), both)
        some, few = jnp.zeros((16, NZ), f32), jnp.zeros((8, NZ), f32)
        s = s + jnp.concatenate([some, wide_rows[128:144], few, wide_rows[144:152], some], axis=0)
        s = jnp.concatenate([s[:, : NZ // 2], s[:, NZ // 2 :]], axis=0)
        for i in range(2):
            sb[group, 128 * i : 128 * i + 128, :] = s[:, 128 * i : 128 * i + 128].T

    def chunk(n):
        return pl.ds(n * OWNED, OWNED)

    place = gy * GX + gx

    def to_owners(group):
        def copy_to(k):
            t = lax.rem(owner + k, OWNERS)
            return pltpu.make_async_remote_copy(
                src_ref=sb.at[group, chunk(t)], dst_ref=rbuf.at[chunk(place)],
                send_sem=a_send.at[group], recv_sem=a_recv.at[0],
                device_id=(lax.div(t, 8), lax.rem(t, 8) * 2 + group), device_id_type=MESH,
            )

        @pl.when(parity != group)
        def _():
            copy_to(0).start()

        @pl.when(parity == group)
        def _():
            pltpu.make_async_copy(sb.at[group, chunk(owner)], rbuf.at[chunk(place)], a_recv.at[0]).start()

        def start(k, carry):
            copy_to(k).start()
            return carry

        lax.fori_loop(1, OWNERS, start, 0)

    def span(ref, chunks, send, recv):
        rows = ref.at[pl.ds(0, chunks * OWNED)]
        return pltpu.make_async_remote_copy(
            src_ref=rows, dst_ref=rows, send_sem=a_send.at[send], recv_sem=a_recv.at[recv],
            device_id=(right_x, gy), device_id_type=MESH,
        )

    loads[3].wait()
    forward(1, cot)
    pl.semaphore_wait(all_sem, GY - 1)
    to_owners(1)

    loads[4].wait()
    for copy in halo:
        copy.wait()
    for c in range(3):
        for x in range(BX):
            vb[c, x + 2, 6:8, :] = yr[0, c, 2 * x : 2 * x + 2, :]
            vb[c, x + 2, 8 + BY : 10 + BY, :] = yr[1, c, 2 * x : 2 * x + 2, :]

    def section_row(x, carry):
        fluid = fluid_at(x)
        kx, ky, kz = weights(adv[0, x]), weights(adv[1, x]), weights(adv[2, x])
        for c in range(3):
            center = vb[c, x + 2, 8 : 8 + BY, :]
            total = center * (kx[0] + ky[0] + kz[0])
            for offset in (-2, -1, 1, 2):
                total = total + kx[offset] * vb[c, x + 2 + offset, 8 : 8 + BY, :]
                total = total + ky[offset] * vb[c, x + 2, 8 + offset : 8 + BY + offset, :]
                total = total + kz[offset] * moved(center, offset, 1)
            sv[c, x] = fluid * (center + scale * total)
        return carry

    lax.fori_loop(0, BX, section_row, 0)
    forward(0, sv)

    to_owners(0)

    loads[5].wait()
    span(rbuf, DEVICES, 0, 0).wait_recv()
    sides = [
        regroup([rbuf[32 * (8 * half + i) : 32 * (8 * half + i) + 32, :] for i in range(8)])
        for half in range(2)
    ]
    rows = [jnp.concatenate([sides[0][j], sides[1][j]], axis=1) for j in range(8)]
    along = dot3(halves(jnp.concatenate([rows[0], rows[4], rows[1], rows[5]], axis=0)), (qy_h[...], qy_l[...]))
    columns = halves(jnp.concatenate([rows[2], rows[6]], axis=0))
    columns = dot(columns[0], order_ref[...]) + dot(columns[1], order_ref[...])
    columns = jnp.concatenate([columns[:, 32 * x : 32 * x + 32] for x in range(BX)], axis=0)
    inner = halves(dot_narrow((large[0], large[1]), halves(columns)))
    along = halves(along)
    left = (
        jnp.concatenate([rw_h[...], inner[0]], axis=1),
        jnp.concatenate([rw_l[...], inner[1]], axis=1),
    )
    right = (
        jnp.concatenate([along[0], wc_h[...]], axis=0),
        jnp.concatenate([along[1], wc_l[...]], axis=0),
    )
    hat = dot3(left, right)
    row = lax.broadcasted_iota(jnp.int32, (512, 128), 0)
    row_mode = lax.rem(row, OWNED) + OWNED * lax.div(row, 256)
    rate = jnp.zeros((512, 128), f32)
    for m in range(2 * OWNED):
        one = rate_s[owner * OWNED + m % OWNED + (NZ // 2) * (m // OWNED)]
        rate = jnp.where(row_mode == m, one, rate)
    hat = halves(hat / (wide(rate + lamx_ref[...], 256) + lamy_ref[...]))
    along = dot3(halves(dot3((rt_h[...], rt_l[...]), hat)), (qt_h[...], qt_l[...]))
    columns = dot_narrow((large[2], large[3]), halves(dot3(hat, (wt_h[...], wt_l[...]))))
    columns = halves(jnp.concatenate([columns[64 * x : 64 * x + 64, :] for x in range(BX)], axis=1))
    columns = dot(columns[0], ordert_ref[...]) + dot(columns[1], ordert_ref[...])
    nothing = jnp.zeros((32, 256), f32)
    rows = [along[0:32], along[64:96], columns[0:32], nothing, along[32:64], along[96:128], columns[32:64], nothing]
    for half in range(2):
        for i, block in enumerate(regroup([r[:, 128 * half : 128 * half + 128] for r in rows])):
            ob[32 * (8 * half + i) : 32 * (8 * half + i) + 32, :] = block

    pltpu.make_async_copy(ob.at[chunk(place)], rb.at[parity, chunk(owner)], a_recv.at[1 + parity]).start()

    def answer(i, carry):
        t = lax.rem(gx * GY + gy + i, DEVICES)
        tx, ty = lax.div(t, GY), lax.rem(t, GY)
        pltpu.make_async_remote_copy(
            src_ref=ob.at[chunk(ty * GX + tx)], dst_ref=rb.at[parity, chunk(owner)],
            send_sem=a_send.at[2], recv_sem=a_recv.at[1 + parity],
            device_id=(tx, ty), device_id_type=MESH,
        ).start()
        return carry

    lax.fori_loop(1, DEVICES, answer, 0)

    def backward(group):
        span(rb.at[group], OWNERS, 0, 1 + group).wait_recv()
        u = jnp.concatenate([rb[group, 0:128, :].T, rb[group, 128:256, :].T], axis=1)
        u = jnp.concatenate([u[0:SLOTS], u[SLOTS:]], axis=1)
        u_parts = halves(u)
        inside = (p1_ref[group] + dot3((nt_h[...], nt_l[...]), u_parts)) * ie_ref[...]
        in_parts = halves(inside)
        both = (
            jnp.concatenate([in_parts[0], u_parts[0]], axis=0),
            jnp.concatenate([in_parts[1], u_parts[1]], axis=0),
        )
        phi = dot3((fs_h[...], fs_l[...]), both)
        ext = jnp.concatenate([phi, u[16:32], u[40:48], jnp.zeros((8, NZ), f32)], axis=0)
        lhs[group] = dot3(halves(ext), (vh[...], vl[...]), nt=True)
        return dot3(halves(phi), (th[...], tl[...]), nt=True)

    def corrections(group, x):
        here = lhs[group, BY * x : BY * x + BY, :]
        after = lhs[group, BY * x + BY : BY * x + 2 * BY, :]
        last = lax.broadcasted_iota(jnp.int32, (BY, NZ), 0) == BY - 1
        side = jnp.where(last, lhs[group, 144 + x : 145 + x, :], jnp.roll(here, -1, 0))
        return here - after, here - side

    tilted = backward(1)
    for x in range(BX):
        fluid = fluid_at(x)
        c0, c1 = corrections(1, x)
        gp[0, x + 2] = fluid * (cot[0, x] - c0)
        gp[1, x + 2] = fluid * (cot[1, x] - c1)
        gp[2, x + 2] = fluid * (cot[2, x] - tilted[BY * x : BY * x + BY])
        sxp[x + 2] = adv[0, x]
    nothing = jnp.zeros((2, BY, NZ), f32)
    for c in range(3):
        gp[c, 0:2] = nothing
        gp[c, BX + 2 : BX + 4] = nothing
    sxp[0:2] = nothing
    sxp[BX + 2 : BX + 4] = nothing

    k0, k1 = weights(adv[0, 0]), weights(adv[0, 1])
    k6, k7 = weights(adv[0, BX - 2]), weights(adv[0, BX - 1])
    for c in range(3):
        g0, g1, g6, g7 = gp[c, 2], gp[c, 3], gp[c, BX], gp[c, BX + 1]
        cxs[0, c, 0] = k0[-2] * g0
        cxs[0, c, 1] = k0[-1] * g0 + k1[-2] * g1
        cxs[1, c, 0] = k7[1] * g7 + k6[2] * g6
        cxs[1, c, 1] = k7[2] * g7
    for x in range(BX):
        k = weights(adv[1, x])
        for c in range(3):
            g = gp[c, x + 2]
            one, two = k[-1] * g, k[-2] * g
            cys[0, c, 2 * x : 2 * x + 1, :] = two[0:1]
            cys[0, c, 2 * x + 1 : 2 * x + 2, :] = one[0:1] + two[1:2]
            one, two = k[1] * g, k[2] * g
            cys[1, c, 2 * x : 2 * x + 1, :] = one[BY - 1 : BY] + two[BY - 2 : BY - 1]
            cys[1, c, 2 * x + 1 : 2 * x + 2, :] = two[BY - 1 : BY]
    edges = [
        remote(cxs.at[0], cxr.at[1], 4, left_x, gy),
        remote(cxs.at[1], cxr.at[0], 5, right_x, gy),
        remote(cys.at[0], cyr.at[1], 6, gx, left_y),
        remote(cys.at[1], cyr.at[0], 7, gx, right_y),
    ]
    for copy in edges:
        copy.start()

    def adjoint_row(x, carry):
        kx = {}
        for offset in (-2, -1, 0, 1, 2):
            kx[offset] = weights(sxp[x + 2 - offset])[offset]
        ky, kz = weights(adv[1, x]), weights(adv[2, x])
        for c in range(3):
            center = gp[c, x + 2]
            total = center * (kx[0] + ky[0] + kz[0])
            for offset in (-2, -1, 1, 2):
                total = total + kx[offset] * gp[c, x + 2 - offset]
                total = total + moved(ky[offset] * center, -offset, 0)
                total = total + moved(kz[offset] * center, -offset, 1)
            adj_ref[c, x] = center + scale * total
        return carry

    lax.fori_loop(0, BX, adjoint_row, 0)

    tilted = backward(0)
    for x in range(BX):
        c0, c1 = corrections(0, x)
        next_ref[0, x] = sv[0, x] - c0
        next_ref[1, x] = sv[1, x] - c1
        next_ref[2, x] = sv[2, x] - tilted[BY * x : BY * x + BY]

    for copy in edges:
        copy.wait()
    for c in range(3):
        for n in range(2):
            adj_ref[c, n] += scale * cxr[0, c, n]
            adj_ref[c, BX - 2 + n] += scale * cxr[1, c, n]
        for x in range(BX):
            adj_ref[c, x, 0:2, :] += scale * cyr[0, c, 2 * x : 2 * x + 2, :]
            adj_ref[c, x, BY - 2 : BY, :] += scale * cyr[1, c, 2 * x : 2 * x + 2, :]

    span(rbuf, DEVICES - 1, 2, 0).wait_send()
    for group in range(2):

        @pl.when(parity != group)
        def _():
            span(rbuf, OWNERS, group, 0).wait_send()

        @pl.when(parity == group)
        def _():
            span(rbuf, OWNERS - 1, group, 0).wait_send()


def per_device(
    velocity_now, advecting, cotangent, building_height, section_index,
    vertical_modes, vertical_tilt, mode_rates,
):
    constants = tables()
    vmem = pl.BlockSpec(memory_space=pltpu.VMEM)
    smem = pl.BlockSpec(memory_space=pltpu.SMEM)
    hbm = pl.BlockSpec(memory_space=pl.ANY)
    field = jax.ShapeDtypeStruct((3, BX, BY, NZ), f32)
    return pl.pallas_call(
        kernel,
        out_shape=(field, field),
        in_specs=[hbm, hbm, hbm, vmem, smem, hbm, hbm, vmem, smem, hbm] + [vmem] * (len(constants) - 1),
        out_specs=(vmem, vmem),
        scratch_shapes=[
            pltpu.VMEM((3, BX + 4, 32, NZ), f32),
            pltpu.VMEM((3, BX, BY, NZ), f32),
            pltpu.VMEM((3, BX, BY, NZ), f32),
            pltpu.VMEM((NZ, NZ), f32),
            pltpu.VMEM((NZ, NZ), f32),
            pltpu.VMEM((4, 512, 512), bf16),
            pltpu.VMEM((3, BX, BY, NZ), f32),
            pltpu.VMEM((2, 160, NZ), f32),
            pltpu.VMEM((NZ, NZ), bf16),
            pltpu.VMEM((NZ, NZ), bf16),
            pltpu.VMEM((NZ, NZ), bf16),
            pltpu.VMEM((NZ, NZ), bf16),
            pltpu.VMEM((2, 3, 16, NZ), f32),
            pltpu.VMEM((2, 3, 16, NZ), f32),
            pltpu.VMEM((2, NZ // 2, 128), f32),
            pltpu.VMEM((NZ, 128), f32),
            pltpu.VMEM((NZ, 128), f32),
            pltpu.VMEM((2, NZ // 2, 128), f32),
            pltpu.VMEM((3, BX + 4, BY, NZ), f32),
            pltpu.VMEM((BX + 4, BY, NZ), f32),
            pltpu.VMEM((2, 3, 2, BY, NZ), f32),
            pltpu.VMEM((2, 3, 2, BY, NZ), f32),
            pltpu.VMEM((2, 3, 16, NZ), f32),
            pltpu.VMEM((2, 3, 16, NZ), f32),
            pltpu.VMEM((2, 128, NZ), f32),
            pltpu.VMEM((128, NZ), f32),
            pltpu.SemaphoreType.DMA((3,)),
            pltpu.SemaphoreType.DMA((3,)),
            pltpu.SemaphoreType.DMA((8,)),
            pltpu.SemaphoreType.DMA((8,)),
            pltpu.SemaphoreType.DMA((6,)),
            pltpu.SemaphoreType.REGULAR,
        ],
        compiler_params=pltpu.CompilerParams(
            collective_id=0, has_side_effects=True, vmem_limit_bytes=56 * 1024 * 1024
        ),
    )(
        velocity_now, advecting, cotangent, building_height, section_index,
        vertical_modes, vertical_tilt, mode_rates.reshape(1, NZ), mode_rates, *constants,
    )


def solution(mesh):
    blocks = P(None, "gx", "gy", None)
    return jax.shard_map(
        per_device,
        mesh=mesh,
        in_specs=(blocks, blocks, blocks, P("gx", "gy"), P(), P(), P(), P()),
        out_specs=(blocks, blocks),
        check_vma=False,
    )
```

```python
import functools
import math

import jax
import jax.numpy as jnp
import ml_dtypes
import numpy as np
from jax import lax
from jax.experimental import pallas as pl
from jax.experimental.pallas import tpu as pltpu
from jax.sharding import PartitionSpec as P

MESH = pl.DeviceIdType.MESH
BX, BY = 8, 16
GX, GY = 8, 16
NX, NY, NZ = 64, 256, 512
DEVICES = GX * GY
OWNERS = DEVICES // 2
OWNED = NZ // OWNERS // 2
SLOTS = 64
LARGE, MID, NARROW = 2304, 992, 688
f32, bf16 = jnp.float32, jnp.bfloat16


def fourier(n):
    place = np.arange(n)
    basis = np.zeros((n, n))
    freq = np.zeros(n)
    for column in range(n):
        k = (column + 1) // 2
        angle = 2.0 * math.pi * k * place / n
        if column == 0 or k == n // 2:
            basis[:, column] = np.cos(angle) / math.sqrt(n)
        else:
            basis[:, column] = (np.cos(angle) if column % 2 else np.sin(angle)) * math.sqrt(2.0 / n)
        freq[column] = 2.0 - 2.0 * math.cos(2.0 * math.pi * k / n)
    return basis, freq


def split_const(matrix, count=2):
    parts = []
    for _ in range(count):
        parts.append(matrix.astype(ml_dtypes.bfloat16))
        matrix = matrix - parts[-1].astype(np.float64)
    return parts


def tables():
    j, k = np.arange(BX), np.arange(BY)
    sin_x = math.sqrt(2.0 / BX) * np.sin(math.pi * np.outer(j, j) / BX)
    sin_y = math.sqrt(2.0 / BY) * np.sin(math.pi * np.outer(k, k) / BY)
    sin_x[0], sin_x[:, 0], sin_y[0], sin_y[:, 0] = 0.0, 0.0, 0.0, 0.0
    sine = np.kron(sin_x, sin_y)
    mu = (2.0 - 2.0 * np.cos(math.pi * j / BX))[:, None] + (2.0 - 2.0 * np.cos(math.pi * k / BY))
    near = np.zeros((SLOTS, BX * BY))
    own = np.zeros((SLOTS, BX * BY))
    for y in range(BY):
        own[y, y] = 1.0
        if y:
            near[y] = sine[1 * BY + y]
            near[16 + y] = sine[(BX - 1) * BY + y]
    for x in range(1, BX):
        own[32 + x, x * BY] = 1.0
        near[32 + x] = sine[x * BY + 1]
        near[40 + x] = sine[x * BY + BY - 1]
    to_slots = np.concatenate([near, own], 1)
    from_slots = np.concatenate([sine, own.T], 1)
    qx, lx = fourier(NX)
    qy, ly = fourier(NY)
    order = np.zeros((GY, 2, BX, BX, 2, GY))
    for g in range(GY):
        for kind in range(2):
            for x in range(BX):
                order[g, kind, x, x, kind, g] = 1.0
    order = order.reshape(256, 256)
    rows = np.zeros((2, NX, OWNED, 2, 2, GX, OWNED))
    cols = np.zeros((2, NX, OWNED, BX, 2, GX, OWNED))
    for group in range(2):
        for mode in range(OWNED):
            for g in range(GX):
                for kind in range(2):
                    rows[group, :, mode, kind, group, g, mode] = qx[8 * (g + kind) % NX]
                for x in range(BX):
                    cols[group, :, mode, x, group, g, mode] = qx[8 * g + x]
    rows = rows.reshape(512, 128)
    cols = cols.reshape(512, 512)
    wc = np.stack([qy[0::16], np.roll(qy[0::16], -1, axis=0)]).reshape(32, 256)
    lam_x = np.broadcast_to(lx[None, :, None], (2, NX, OWNED)).reshape(512)

    def columns(values):
        out = np.zeros((values.size, 128), ml_dtypes.bfloat16)
        for n, part in enumerate(split_const(values.reshape(-1), 3)):
            out[:, n] = part
        return out

    def packed(matrices, lanes):
        parts = []
        for matrix in matrices:
            for part in split_const(np.ascontiguousarray(matrix)):
                parts.append(np.pad(part, ((0, 0), (0, lanes - part.shape[1]))))
        return np.concatenate(parts)

    exact = np.concatenate([order, order.T]).astype(ml_dtypes.bfloat16)
    lam_y = np.stack(split_const(ly, 3)).reshape(6, 128)
    large = packed([cols, cols.T, rows.T], 512)
    mid = np.concatenate([exact, packed([qy, qy.T, wc, to_slots, from_slots], 256)])
    narrow = np.concatenate([packed([sine, rows, near.T, wc.T], 128), columns(lam_x), columns(mu), lam_y])
    narrow = np.pad(narrow, ((0, 4 * NARROW - narrow.shape[0]), (0, 0)))
    mid = np.concatenate([mid[:MID], mid[MID:]], axis=1)
    narrow = np.concatenate([narrow[NARROW * i : NARROW * i + NARROW] for i in range(4)], axis=1)
    return jnp.asarray(np.concatenate([large, mid, narrow]))


def summed(parts):
    parts = parts.astype(f32)
    return parts[:, 0:1] + (parts[:, 1:2] + parts[:, 2:3])


def unpacked(ref, start, rows, lanes):
    return ref[start : start + rows, :lanes], ref[start + rows : start + 2 * rows, :lanes]


def halves(value):
    high = value.astype(bf16)
    low = (value - high.astype(f32)).astype(bf16)
    return high, low


def dot(a, b, nt=False):
    dims = (((1,), (1 if nt else 0,)), ((), ()))
    return lax.dot_general(a, b, dims, preferred_element_type=f32)


def dot_narrow(a, b):
    n = b[0].shape[1]
    both = dot(a[0], jnp.concatenate([b[0], b[1]], axis=1))
    return both[:, :n] + (both[:, n:] + dot(a[1], b[0]))


def regroup(blocks):
    blocks = list(blocks)
    group = lax.broadcasted_iota(jnp.int32, blocks[0].shape, 1) // 16
    for step in (4, 2, 1):
        low = (group & step) == 0
        for i in range(8):
            if not i & step:
                a, b = blocks[i], blocks[i + step]
                blocks[i] = jnp.where(low, a, pltpu.roll(b, 16 * step, 1))
                blocks[i + step] = jnp.where(low, pltpu.roll(a, 128 - 16 * step, 1), b)
    return blocks


def dot3(a, b, nt=False):
    return dot(a[0], b[0], nt) + (dot(a[0], b[1], nt) + dot(a[1], b[0], nt))


def wide(column, lanes):
    return jnp.concatenate([column] * (lanes // 128), axis=1)


TAPS = ((-2, 1.0, 1.0), (-1, -8.0, -4.0), (0, 0.0, 6.0), (1, 8.0, -4.0), (2, -1.0, 1.0))


def weights(speed):
    size = jnp.abs(speed)
    out = {}
    for offset, central, hyper in TAPS:
        out[offset] = hyper * size + central * speed if central else hyper * size
    return out


def moved(value, offset, axis):
    n = value.shape[axis]
    if axis == 1:
        rolled = pltpu.roll(value, (-offset) % n, 1)
    else:
        rolled = jnp.roll(value, -offset, 0)
    place = lax.broadcasted_iota(jnp.int32, value.shape, axis)
    keep = place < n - offset if offset > 0 else place >= -offset
    return jnp.where(keep, rolled, 0.0)


def kernel(
    vel_h, adv_h, cot_h, small, vm_h, vt_h, tables_h,
    next_ref, adj_ref,
    vb, adv, cot, vm_ref, vt_ref, large, mid, narrow,
    sv, lhs, vh, vl, th, tl, ys, yr, sb, rbuf, ob, rb, gp, sxp, cxs, cxr, cys, cyr,
    p1_ref, ie_ref,
    a_send, a_recv, h_send, h_recv, l_sem, all_sem,
):
    gx, gy = lax.axis_index("gx"), lax.axis_index("gy")
    me = gx * GY + gy
    left_x, right_x = lax.rem(gx + GX - 1, GX), lax.rem(gx + 1, GX)
    left_y, right_y = lax.rem(gy + GY - 1, GY), lax.rem(gy + 1, GY)

    parity, half_y = lax.rem(gy, 2), lax.div(gy, 2)
    owner = gx * 8 + half_y
    barrier = pltpu.get_barrier_semaphore()
    for i in range(1, GX):
        pl.semaphore_signal(barrier, inc=1, device_id=(lax.rem(gx + i, GX), gy), device_id_type=MESH)
    for i in range(1, GY):
        pl.semaphore_signal(barrier, inc=1, device_id=(gx, lax.rem(gy + i, GY)), device_id_type=MESH)

    loads = [
        pltpu.make_async_copy(source, target, l_sem.at[n])
        for n, (source, target) in enumerate(
            (
                (vel_h, vb.at[:, pl.ds(2, BX), pl.ds(8, BY)]),
                (vm_h, vm_ref),
                (vt_h, vt_ref),
                (cot_h, cot),
                (adv_h, adv),
                (tables_h.at[pl.ds(0, LARGE)], large),
            )
            + tuple(
                (tables_h.at[pl.ds(LARGE + MID, NARROW), pl.ds(128 * i, 128)], narrow.at[pl.ds(NARROW * i, NARROW)])
                for i in range(4)
            )
            + tuple(
                (tables_h.at[pl.ds(LARGE, MID), pl.ds(256 * i, 256)], mid.at[pl.ds(MID * i, MID)])
                for i in range(2)
            )
        )
    ]
    for n in (0, 3, 1, 2, 6, 7, 8, 9, 10, 11, 4, 5):
        loads[n].start()
    loads[0].wait()

    for c in range(3):
        for x in range(BX):
            ys[0, c, 2 * x : 2 * x + 2, :] = vb[c, x + 2, 8:10, :]
            ys[1, c, 2 * x : 2 * x + 2, :] = vb[c, x + 2, 6 + BY : 8 + BY, :]

    pl.semaphore_wait(barrier, GX + GY - 2)

    def remote(src, dst, n, x, y):
        return pltpu.make_async_remote_copy(
            src_ref=src, dst_ref=dst, send_sem=h_send.at[n], recv_sem=h_recv.at[n],
            device_id=(x, y), device_id_type=MESH,
        )

    halo = [
        remote(vel_h.at[:, pl.ds(0, 2)], vb.at[:, pl.ds(BX + 2, 2), pl.ds(8, BY)], 0, left_x, gy),
        remote(vel_h.at[:, pl.ds(BX - 2, 2)], vb.at[:, pl.ds(0, 2), pl.ds(8, BY)], 1, right_x, gy),
        remote(ys.at[0], yr.at[1], 2, gx, left_y),
        remote(ys.at[1], yr.at[0], 3, gx, right_y),
    ]
    for n in (2, 3, 0, 1):
        halo[n].start()

    for i in range(1, GY):
        pl.semaphore_signal(all_sem, inc=1, device_id=(gx, lax.rem(gy + i, GY)), device_id_type=MESH)

    loads[1].wait()
    loads[2].wait()
    for full, high, low in ((vm_ref, vh, vl), (vt_ref, th, tl)):
        for i in range(0, NZ, 64):
            h, l = halves(full[i : i + 64, :])
            high[i : i + 64, :] = h
            low[i : i + 64, :] = l
    for n in range(6, 10):
        loads[n].wait()
    rate_row = jnp.concatenate([small[n : n + 1, :] for n in range(4)], axis=1)
    ie_ref[...] = 1.0 / (summed(narrow[2560:2688, :]) + rate_row)

    factor = small[4:5, 0:1]
    scale = factor * f32(-1.0 / 12.0)

    levels = lax.broadcasted_iota(jnp.int32, (BY, NZ), 1).astype(f32)
    diagonal = lax.broadcasted_iota(jnp.int32, (BY, BY), 0) == lax.broadcasted_iota(
        jnp.int32, (BY, BY), 1
    )

    def fluid_at(x):
        row = small[pl.ds(8 + x, 1), 0:BY]
        column = jnp.sum(jnp.where(diagonal, row, 0.0), axis=1, keepdims=True)
        return (levels >= column).astype(f32)

    def left_sides(group, field):
        for x in range(BX):
            f0 = field[0, x]
            if x:
                f0 = f0 - field[0, x - 1]
            f1 = field[1, x]
            lhs[group, BY * x : BY * x + BY, :] = f0 + (f1 - moved(f1, -1, 0))
            lhs[group, 144 + x : 145 + x, :] = -field[1, x, BY - 1 : BY, :]
        lhs[group, 128:144, :] = -field[0, BX - 1]
        lhs[group, 152:160, :] = jnp.zeros((8, NZ), f32)

    def forward(group, field):
        left_sides(group, field)
        wide_rows = dot3(halves(lhs[group]), (vh[...], vl[...]))
        tilted = dot3(halves(field[2].reshape(BX * BY, NZ)), (th[...], tl[...]))
        d = wide_rows[:128] + tilted
        d_parts = halves(d)
        p1 = dot3(unpacked(narrow, 0, 128, 128), d_parts)
        p1_ref[group] = p1
        w = halves(p1 * ie_ref[...])
        both = (
            jnp.concatenate([w[0], d_parts[0]], axis=0),
            jnp.concatenate([w[1], d_parts[1]], axis=0),
        )
        s = dot3(unpacked(mid, 1600, 64, 256), both)
        some, few = jnp.zeros((16, NZ), f32), jnp.zeros((8, NZ), f32)
        s = s + jnp.concatenate([some, wide_rows[128:144], few, wide_rows[144:152], some], axis=0)
        s = jnp.concatenate([s[:, : NZ // 2], s[:, NZ // 2 :]], axis=0)
        for i in range(2):
            sb[group, 128 * i : 128 * i + 128, :] = s[:, 128 * i : 128 * i + 128].T

    def chunk(n):
        return pl.ds(n * OWNED, OWNED)

    place = gy * GX + gx

    def to_owners(group):
        def copy_to(dx, dy):
            tx, ty = lax.rem(gx + dx, GX), lax.rem(half_y + dy, 8)
            return pltpu.make_async_remote_copy(
                src_ref=sb.at[group, chunk(tx * 8 + ty)], dst_ref=rbuf.at[chunk(place)],
                send_sem=a_send.at[group], recv_sem=a_recv.at[0],
                device_id=(tx, ty * 2 + group), device_id_type=MESH,
            )

        @pl.when(parity != group)
        def _():
            copy_to(0, 0).start()

        @pl.when(parity == group)
        def _():
            pltpu.make_async_copy(sb.at[group, chunk(owner)], rbuf.at[chunk(place)], a_recv.at[0]).start()

        def start(dx, carry):
            for dy in range(8):
                copy_to(dx, dy).start()
            return carry

        for dy in range(1, 8):
            copy_to(0, dy).start()
        lax.fori_loop(1, GX, start, 0)

    def span(ref, chunks, send, recv):
        rows = ref.at[pl.ds(0, chunks * OWNED)]
        return pltpu.make_async_remote_copy(
            src_ref=rows, dst_ref=rows, send_sem=a_send.at[send], recv_sem=a_recv.at[recv],
            device_id=(right_x, gy), device_id_type=MESH,
        )

    loads[3].wait()
    loads[10].wait()
    loads[11].wait()
    forward(1, cot)
    pl.semaphore_wait(all_sem, GY - 1)
    to_owners(1)

    loads[4].wait()
    halo[2].wait()
    halo[3].wait()
    for c in range(3):
        for x in range(BX):
            vb[c, x + 2, 6:8, :] = yr[0, c, 2 * x : 2 * x + 2, :]
            vb[c, x + 2, 8 + BY : 10 + BY, :] = yr[1, c, 2 * x : 2 * x + 2, :]

    def section_row(x, carry):
        fluid = fluid_at(x)
        kx, ky, kz = weights(adv[0, x]), weights(adv[1, x]), weights(adv[2, x])
        for c in range(3):
            center = vb[c, x + 2, 8 : 8 + BY, :]
            total = center * (kx[0] + ky[0] + kz[0])
            for offset in (-2, -1, 1, 2):
                total = total + kx[offset] * vb[c, x + 2 + offset, 8 : 8 + BY, :]
                total = total + ky[offset] * vb[c, x + 2, 8 + offset : 8 + BY + offset, :]
                total = total + kz[offset] * moved(center, offset, 1)
            sv[c, x] = fluid * (center + scale * total)
        return carry

    lax.fori_loop(2, BX - 2, section_row, 0)
    halo[0].wait()
    halo[1].wait()
    lax.fori_loop(0, 2, section_row, 0)
    lax.fori_loop(BX - 2, BX, section_row, 0)
    forward(0, sv)

    to_owners(0)

    loads[5].wait()
    span(rbuf, DEVICES, 0, 0).wait_recv()
    sides = [
        regroup([rbuf[32 * (8 * half + i) : 32 * (8 * half + i) + 32, :] for i in range(8)])
        for half in range(2)
    ]
    rows = [jnp.concatenate([sides[0][j], sides[1][j]], axis=1) for j in range(8)]
    along = dot3(halves(jnp.concatenate([rows[0], rows[4], rows[1], rows[5]], axis=0)), unpacked(mid, 512, 256, 256))
    columns = halves(jnp.concatenate([rows[2], rows[6]], axis=0))
    columns = dot(columns[0], mid[0:256, :]) + dot(columns[1], mid[0:256, :])
    columns = jnp.concatenate([columns[:, 32 * x : 32 * x + 32] for x in range(BX)], axis=0)
    inner = halves(dot_narrow(unpacked(large, 0, 512, 512), halves(columns)))
    along = halves(along)
    row_table, edge_table = unpacked(narrow, 256, 512, 128), unpacked(mid, 1536, 32, 256)
    left = [jnp.concatenate([row_table[i], inner[i]], axis=1) for i in range(2)]
    right = [jnp.concatenate([along[i], edge_table[i]], axis=0) for i in range(2)]
    hat = dot3(left, right)
    row = lax.broadcasted_iota(jnp.int32, (512, 128), 0)
    row_mode = lax.rem(row, OWNED) + OWNED * lax.div(row, 256)
    rate = jnp.zeros((512, 128), f32)
    lane = lax.broadcasted_iota(jnp.int32, (1, 128), 1)
    first_lane = lax.rem(owner, 128 // OWNED) * OWNED
    for half in range(2):
        rates = small[pl.ds(2 * half + lax.div(owner, 128 // OWNED), 1), :]
        for m in range(OWNED):
            one = jnp.sum(jnp.where(lane == first_lane + m, rates, 0.0), axis=1, keepdims=True)
            rate = jnp.where(row_mode == OWNED * half + m, one, rate)
    lam_y = narrow[2688:2704, :].astype(f32)
    lam_y = [lam_y[n : n + 1] + (lam_y[n + 2 : n + 3] + lam_y[n + 4 : n + 5]) for n in range(2)]
    lam_y = jnp.concatenate(lam_y, axis=1)
    hat = halves(hat / (wide(rate + summed(narrow[2048:2560, :]), 256) + lam_y))
    along = dot3(halves(dot3(unpacked(large, 2048, 128, 512), hat)), unpacked(mid, 1024, 256, 256))
    columns = dot_narrow(unpacked(large, 1024, 512, 512), halves(dot3(hat, unpacked(narrow, 1536, 256, 32))))
    columns = halves(jnp.concatenate([columns[64 * x : 64 * x + 64, :] for x in range(BX)], axis=1))
    columns = dot(columns[0], mid[256:512, :]) + dot(columns[1], mid[256:512, :])
    nothing = jnp.zeros((32, 256), f32)
    rows = [along[0:32], along[64:96], columns[0:32], nothing, along[32:64], along[96:128], columns[32:64], nothing]
    for half in range(2):
        for i, block in enumerate(regroup([r[:, 128 * half : 128 * half + 128] for r in rows])):
            ob[32 * (8 * half + i) : 32 * (8 * half + i) + 32, :] = block

    pltpu.make_async_copy(ob.at[chunk(place)], rb.at[parity, chunk(owner)], a_recv.at[1 + parity]).start()

    def answer(dx, dy):
        tx, ty = lax.rem(gx + dx, GX), lax.rem(gy + dy, GY)
        pltpu.make_async_remote_copy(
            src_ref=ob.at[chunk(ty * GX + tx)], dst_ref=rb.at[parity, chunk(owner)],
            send_sem=a_send.at[2], recv_sem=a_recv.at[1 + parity],
            device_id=(tx, ty), device_id_type=MESH,
        ).start()

    def answers(dx, carry):
        for dy in range(GY):
            answer(dx, dy)
        return carry

    for dy in range(1, GY):
        answer(0, dy)
    lax.fori_loop(1, GX, answers, 0)

    def backward(group):
        span(rb.at[group], OWNERS, 0, 1 + group).wait_recv()
        u = jnp.concatenate([rb[group, 0:128, :].T, rb[group, 128:256, :].T], axis=1)
        u = jnp.concatenate([u[0:SLOTS], u[SLOTS:]], axis=1)
        u_parts = halves(u)
        inside = (p1_ref[group] + dot3(unpacked(narrow, 1280, 128, 64), u_parts)) * ie_ref[...]
        in_parts = halves(inside)
        both = (
            jnp.concatenate([in_parts[0], u_parts[0]], axis=0),
            jnp.concatenate([in_parts[1], u_parts[1]], axis=0),
        )
        phi = dot3(unpacked(mid, 1728, 128, 192), both)
        ext = jnp.concatenate([phi, u[16:32], u[40:48], jnp.zeros((8, NZ), f32)], axis=0)
        lhs[group] = dot3(halves(ext), (vh[...], vl[...]), nt=True)
        return dot3(halves(phi), (th[...], tl[...]), nt=True)

    def corrections(group, x):
        here = lhs[group, BY * x : BY * x + BY, :]
        after = lhs[group, BY * x + BY : BY * x + 2 * BY, :]
        last = lax.broadcasted_iota(jnp.int32, (BY, NZ), 0) == BY - 1
        side = jnp.where(last, lhs[group, 144 + x : 145 + x, :], jnp.roll(here, -1, 0))
        return here - after, here - side

    tilted = backward(1)

    def gradient_row(x):
        fluid = fluid_at(x)
        c0, c1 = corrections(1, x)
        gp[0, x + 2] = fluid * (cot[0, x] - c0)
        gp[1, x + 2] = fluid * (cot[1, x] - c1)
        gp[2, x + 2] = fluid * (cot[2, x] - tilted[BY * x : BY * x + BY])
        sxp[x + 2] = adv[0, x]

    for x in (0, 1, BX - 2, BX - 1):
        gradient_row(x)

    k0, k1 = weights(adv[0, 0]), weights(adv[0, 1])
    k6, k7 = weights(adv[0, BX - 2]), weights(adv[0, BX - 1])
    for c in range(3):
        g0, g1, g6, g7 = gp[c, 2], gp[c, 3], gp[c, BX], gp[c, BX + 1]
        cxs[0, c, 0] = k0[-2] * g0
        cxs[0, c, 1] = k0[-1] * g0 + k1[-2] * g1
        cxs[1, c, 0] = k7[1] * g7 + k6[2] * g6
        cxs[1, c, 1] = k7[2] * g7
    edges = [
        remote(cxs.at[0], cxr.at[1], 4, left_x, gy),
        remote(cxs.at[1], cxr.at[0], 5, right_x, gy),
        remote(cys.at[0], cyr.at[1], 6, gx, left_y),
        remote(cys.at[1], cyr.at[0], 7, gx, right_y),
    ]
    edges[0].start()
    edges[1].start()
    for x in range(2, BX - 2):
        gradient_row(x)
    for x in range(BX):
        k = weights(adv[1, x])
        for c in range(3):
            g = gp[c, x + 2]
            one, two = k[-1] * g, k[-2] * g
            cys[0, c, 2 * x : 2 * x + 1, :] = two[0:1]
            cys[0, c, 2 * x + 1 : 2 * x + 2, :] = one[0:1] + two[1:2]
            one, two = k[1] * g, k[2] * g
            cys[1, c, 2 * x : 2 * x + 1, :] = one[BY - 1 : BY] + two[BY - 2 : BY - 1]
            cys[1, c, 2 * x + 1 : 2 * x + 2, :] = two[BY - 1 : BY]
    edges[2].start()
    edges[3].start()
    nothing = jnp.zeros((2, BY, NZ), f32)
    for c in range(3):
        gp[c, 0:2] = nothing
        gp[c, BX + 2 : BX + 4] = nothing
    sxp[0:2] = nothing
    sxp[BX + 2 : BX + 4] = nothing

    def adjoint_row(x, carry):
        kx = {}
        for offset in (-2, -1, 0, 1, 2):
            kx[offset] = weights(sxp[x + 2 - offset])[offset]
        ky, kz = weights(adv[1, x]), weights(adv[2, x])
        for c in range(3):
            center = gp[c, x + 2]
            total = center * (kx[0] + ky[0] + kz[0])
            for offset in (-2, -1, 1, 2):
                total = total + kx[offset] * gp[c, x + 2 - offset]
                total = total + moved(ky[offset] * center, -offset, 0)
                total = total + moved(kz[offset] * center, -offset, 1)
            adj_ref[c, x] = center + scale * total
        return carry

    lax.fori_loop(0, BX, adjoint_row, 0)

    tilted = backward(0)
    for x in range(BX):
        c0, c1 = corrections(0, x)
        next_ref[0, x] = sv[0, x] - c0
        next_ref[1, x] = sv[1, x] - c1
        next_ref[2, x] = sv[2, x] - tilted[BY * x : BY * x + BY]

    for copy in edges:
        copy.wait()
    for c in range(3):
        for n in range(2):
            adj_ref[c, n] += scale * cxr[0, c, n]
            adj_ref[c, BX - 2 + n] += scale * cxr[1, c, n]
        for x in range(BX):
            adj_ref[c, x, 0:2, :] += scale * cyr[0, c, 2 * x : 2 * x + 2, :]
            adj_ref[c, x, BY - 2 : BY, :] += scale * cyr[1, c, 2 * x : 2 * x + 2, :]

    span(rbuf, DEVICES - 1, 2, 0).wait_send()
    for group in range(2):

        @pl.when(parity != group)
        def _():
            span(rbuf, OWNERS, group, 0).wait_send()

        @pl.when(parity == group)
        def _():
            span(rbuf, OWNERS - 1, group, 0).wait_send()


def section_factor(section_index):
    section = lax.rem(section_index[0], 3)
    step = lax.div(section_index[0], 3).astype(f32)
    size = f32(0.2) + f32(0.2) * step / f32(63.0)
    return size * jnp.where(section == 0, f32(1.0 / 3.0), jnp.where(section == 1, f32(0.5), f32(1.0)))


def per_device(
    velocity_now, advecting, cotangent, building_height, section_index,
    vertical_modes, vertical_tilt, mode_rates,
):
    small = jnp.concatenate(
        [
            mode_rates.reshape(4, 128),
            jnp.broadcast_to(section_factor(section_index), (4, 128)),
            jnp.pad(building_height, ((0, 0), (0, 128 - BY))).astype(f32),
        ]
    )
    vmem = pl.BlockSpec(memory_space=pltpu.VMEM)
    hbm = pl.BlockSpec(memory_space=pltpu.HBM)
    field = jax.ShapeDtypeStruct((3, BX, BY, NZ), f32)
    return pl.pallas_call(
        kernel,
        out_shape=(field, field),
        in_specs=[hbm, hbm, hbm, vmem, hbm, hbm, hbm],
        out_specs=(vmem, vmem),
        scratch_shapes=[
            pltpu.VMEM((3, BX + 4, 32, NZ), f32),
            pltpu.VMEM((3, BX, BY, NZ), f32),
            pltpu.VMEM((3, BX, BY, NZ), f32),
            pltpu.VMEM((NZ, NZ), f32),
            pltpu.VMEM((NZ, NZ), f32),
            pltpu.VMEM((LARGE, 512), bf16),
            pltpu.VMEM((2 * MID, 256), bf16),
            pltpu.VMEM((4 * NARROW, 128), bf16),
            pltpu.VMEM((3, BX, BY, NZ), f32),
            pltpu.VMEM((2, 160, NZ), f32),
            pltpu.VMEM((NZ, NZ), bf16),
            pltpu.VMEM((NZ, NZ), bf16),
            pltpu.VMEM((NZ, NZ), bf16),
            pltpu.VMEM((NZ, NZ), bf16),
            pltpu.VMEM((2, 3, 16, NZ), f32),
            pltpu.VMEM((2, 3, 16, NZ), f32),
            pltpu.VMEM((2, NZ // 2, 128), f32),
            pltpu.VMEM((NZ, 128), f32),
            pltpu.VMEM((NZ, 128), f32),
            pltpu.VMEM((2, NZ // 2, 128), f32),
            pltpu.VMEM((3, BX + 4, BY, NZ), f32),
            pltpu.VMEM((BX + 4, BY, NZ), f32),
            pltpu.VMEM((2, 3, 2, BY, NZ), f32),
            pltpu.VMEM((2, 3, 2, BY, NZ), f32),
            pltpu.VMEM((2, 3, 16, NZ), f32),
            pltpu.VMEM((2, 3, 16, NZ), f32),
            pltpu.VMEM((2, 128, NZ), f32),
            pltpu.VMEM((128, NZ), f32),
            pltpu.SemaphoreType.DMA((3,)),
            pltpu.SemaphoreType.DMA((3,)),
            pltpu.SemaphoreType.DMA((8,)),
            pltpu.SemaphoreType.DMA((8,)),
            pltpu.SemaphoreType.DMA((12,)),
            pltpu.SemaphoreType.REGULAR,
        ],
        compiler_params=pltpu.CompilerParams(
            collective_id=0, has_side_effects=True, vmem_limit_bytes=52 * 1024 * 1024
        ),
    )(
        velocity_now, advecting, cotangent, small, vertical_modes, vertical_tilt, tables(),
    )


def solution(mesh):
    blocks = P(None, "gx", "gy", None)
    return jax.shard_map(
        per_device,
        mesh=mesh,
        in_specs=(blocks, blocks, blocks, P("gx", "gy"), P(), P(), P(), P()),
        out_specs=(blocks, blocks),
        check_vma=False,
    )
```

```python
import functools
import math

import jax
import jax.numpy as jnp
import ml_dtypes
import numpy as np
from jax import lax
from jax.experimental import pallas as pl
from jax.experimental.pallas import tpu as pltpu
from jax.sharding import PartitionSpec as P

MESH = pl.DeviceIdType.MESH
BX, BY = 8, 16
GX, GY = 8, 16
NX, NY, NZ = 64, 256, 512
DEVICES = GX * GY
OWNERS = DEVICES // 2
OWNED = NZ // OWNERS // 2
SLOTS = 64
LARGE, MID, NARROW = 256, 992, 752
f32, bf16 = jnp.float32, jnp.bfloat16


def fourier(n):
    place = np.arange(n)
    basis = np.zeros((n, n))
    freq = np.zeros(n)
    for column in range(n):
        k = (column + 1) // 2
        angle = 2.0 * math.pi * k * place / n
        if column == 0 or k == n // 2:
            basis[:, column] = np.cos(angle) / math.sqrt(n)
        else:
            basis[:, column] = (np.cos(angle) if column % 2 else np.sin(angle)) * math.sqrt(2.0 / n)
        freq[column] = 2.0 - 2.0 * math.cos(2.0 * math.pi * k / n)
    return basis, freq


def split_const(matrix, count=2):
    parts = []
    for _ in range(count):
        parts.append(matrix.astype(ml_dtypes.bfloat16))
        matrix = matrix - parts[-1].astype(np.float64)
    return parts


def tables():
    j, k = np.arange(BX), np.arange(BY)
    sin_x = math.sqrt(2.0 / BX) * np.sin(math.pi * np.outer(j, j) / BX)
    sin_y = math.sqrt(2.0 / BY) * np.sin(math.pi * np.outer(k, k) / BY)
    sin_x[0], sin_x[:, 0], sin_y[0], sin_y[:, 0] = 0.0, 0.0, 0.0, 0.0
    sine = np.kron(sin_x, sin_y)
    mu = (2.0 - 2.0 * np.cos(math.pi * j / BX))[:, None] + (2.0 - 2.0 * np.cos(math.pi * k / BY))
    near = np.zeros((SLOTS, BX * BY))
    own = np.zeros((SLOTS, BX * BY))
    for y in range(BY):
        own[y, y] = 1.0
        if y:
            near[y] = sine[1 * BY + y]
            near[16 + y] = sine[(BX - 1) * BY + y]
    for x in range(1, BX):
        own[32 + x, x * BY] = 1.0
        near[32 + x] = sine[x * BY + 1]
        near[40 + x] = sine[x * BY + BY - 1]
    to_slots = np.concatenate([near, own], 1)
    from_slots = np.concatenate([sine, own.T], 1)
    qx, lx = fourier(NX)
    qy, ly = fourier(NY)
    order = np.zeros((GY, 2, BX, BX, 2, GY))
    for g in range(GY):
        for kind in range(2):
            for x in range(BX):
                order[g, kind, x, x, kind, g] = 1.0
    order = order.reshape(256, 256)
    rows = np.zeros((2, OWNED, NX, 2, 2, GX, OWNED))
    for group in range(2):
        for mode in range(OWNED):
            for g in range(GX):
                for kind in range(2):
                    rows[group, mode, :, kind, group, g, mode] = qx[8 * (g + kind) % NX]
    rows = rows.reshape(512, 128)
    cols = qx.reshape(GX, BX, NX).transpose(2, 1, 0).reshape(NX, NX)
    wc = np.stack([qy[0::16], np.roll(qy[0::16], -1, axis=0)]).reshape(32, 256)
    lam_x = np.tile(lx, 2 * OWNED)

    def columns(values):
        out = np.zeros((values.size, 128), ml_dtypes.bfloat16)
        for n, part in enumerate(split_const(values.reshape(-1), 3)):
            out[:, n] = part
        return out

    def packed(matrices, lanes):
        parts = []
        for matrix in matrices:
            for part in split_const(np.ascontiguousarray(matrix)):
                parts.append(np.pad(part, ((0, 0), (0, lanes - part.shape[1]))))
        return np.concatenate(parts)

    exact = np.concatenate([order, order.T]).astype(ml_dtypes.bfloat16)
    lam_y = np.stack(split_const(ly, 3)).reshape(6, 128)
    large = packed([rows.T], 512)
    mid = np.concatenate([exact, packed([qy, qy.T, wc, to_slots, from_slots], 256)])
    narrow = np.concatenate([packed([sine, rows, near.T, wc.T, cols, cols.T], 128), columns(lam_x), columns(mu), lam_y])
    narrow = np.pad(narrow, ((0, 4 * NARROW - narrow.shape[0]), (0, 0)))
    mid = np.concatenate([mid[:MID], mid[MID:]], axis=1)
    narrow = np.concatenate([narrow[NARROW * i : NARROW * i + NARROW] for i in range(4)], axis=1)
    return jnp.asarray(np.concatenate([large, mid, narrow]))


def summed(parts):
    parts = parts.astype(f32)
    return parts[:, 0:1] + (parts[:, 1:2] + parts[:, 2:3])


def unpacked(ref, start, rows, lanes):
    return ref[start : start + rows, :lanes], ref[start + rows : start + 2 * rows, :lanes]


def halves(value):
    high = value.astype(bf16)
    low = (value - high.astype(f32)).astype(bf16)
    return high, low


def dot(a, b, nt=False):
    dims = (((1,), (1 if nt else 0,)), ((), ()))
    return lax.dot_general(a, b, dims, preferred_element_type=f32)


def regroup(blocks):
    blocks = list(blocks)
    lanes = 128 // len(blocks)
    group = lax.broadcasted_iota(jnp.int32, blocks[0].shape, 1) // lanes
    step = len(blocks) // 2
    while step:
        low = (group & step) == 0
        for i in range(len(blocks)):
            if not i & step:
                a, b = blocks[i], blocks[i + step]
                blocks[i] = jnp.where(low, a, pltpu.roll(b, lanes * step, 1))
                blocks[i + step] = jnp.where(low, pltpu.roll(a, 128 - lanes * step, 1), b)
        step //= 2
    return blocks


def regroup_wide(blocks):
    out = []
    for right in range(2):
        quads = [regroup([b[:, 128 * right : 128 * right + 128] for b in blocks[4 * n : 4 * n + 4]]) for n in range(2)]
        out.extend(jnp.concatenate([a, b], axis=1) for a, b in zip(*quads))
    return out


def dot3(a, b, nt=False):
    n = a[0].shape[0]
    both = dot(jnp.concatenate([a[0], a[1]], axis=0), b[0], nt)
    return both[:n] + (dot(a[0], b[1], nt) + both[n:])


def wide(column, lanes):
    return jnp.concatenate([column] * (lanes // 128), axis=1)


TAPS = ((-2, 1.0, 1.0), (-1, -8.0, -4.0), (0, 0.0, 6.0), (1, 8.0, -4.0), (2, -1.0, 1.0))


def weights(speed):
    size = jnp.abs(speed)
    out = {}
    for offset, central, hyper in TAPS:
        out[offset] = hyper * size + central * speed if central else hyper * size
    return out


def moved(value, offset, axis):
    n = value.shape[axis]
    if axis == 1:
        rolled = pltpu.roll(value, (-offset) % n, 1)
    else:
        rolled = jnp.roll(value, -offset, 0)
    place = lax.broadcasted_iota(jnp.int32, value.shape, axis)
    keep = place < n - offset if offset > 0 else place >= -offset
    return jnp.where(keep, rolled, 0.0)


def kernel(
    vel_h, adv_h, cot_h, small, vm_h, vt_h, tables_h,
    next_ref, adj_ref,
    vb, adv, cot, vm_ref, vt_ref, large, mid, narrow,
    sv, lhs, vh, vl, th, tl, ys, yr, sb, rbuf, ob, rb, gp, sxp, cxs, cxr, cys, cyr,
    p1_ref, ie_ref, cs,
    a_send, a_recv, h_send, h_recv, l_sem, all_sem,
):
    gx, gy = lax.axis_index("gx"), lax.axis_index("gy")
    me = gx * GY + gy
    left_x, right_x = lax.rem(gx + GX - 1, GX), lax.rem(gx + 1, GX)
    left_y, right_y = lax.rem(gy + GY - 1, GY), lax.rem(gy + 1, GY)

    parity, half_y = lax.rem(gy, 2), lax.div(gy, 2)
    owner = gx * 8 + half_y
    barrier = pltpu.get_barrier_semaphore()
    for i in range(1, GX):
        pl.semaphore_signal(barrier, inc=1, device_id=(lax.rem(gx + i, GX), gy), device_id_type=MESH)
    for i in range(1, GY):
        pl.semaphore_signal(barrier, inc=1, device_id=(gx, lax.rem(gy + i, GY)), device_id_type=MESH)

    loads = [
        pltpu.make_async_copy(source, target, l_sem.at[n])
        for n, (source, target) in enumerate(
            (
                (vel_h, vb.at[:, pl.ds(2, BX), pl.ds(8, BY)]),
                (vm_h, vm_ref),
                (vt_h, vt_ref),
                (cot_h, cot),
                (adv_h, adv),
                (tables_h.at[pl.ds(0, LARGE)], large),
            )
            + tuple(
                (tables_h.at[pl.ds(LARGE + MID, NARROW), pl.ds(128 * i, 128)], narrow.at[pl.ds(NARROW * i, NARROW)])
                for i in range(4)
            )
            + tuple(
                (tables_h.at[pl.ds(LARGE, MID), pl.ds(256 * i, 256)], mid.at[pl.ds(MID * i, MID)])
                for i in range(2)
            )
        )
    ]
    for n in (0, 3, 1, 2, 6, 7, 8, 9, 10, 11, 4, 5):
        loads[n].start()
    loads[0].wait()

    for c in range(3):
        for x in range(BX):
            ys[0, c, 2 * x : 2 * x + 2, :] = vb[c, x + 2, 8:10, :]
            ys[1, c, 2 * x : 2 * x + 2, :] = vb[c, x + 2, 6 + BY : 8 + BY, :]

    pl.semaphore_wait(barrier, GX + GY - 2)

    def remote(src, dst, n, x, y):
        return pltpu.make_async_remote_copy(
            src_ref=src, dst_ref=dst, send_sem=h_send.at[n], recv_sem=h_recv.at[n],
            device_id=(x, y), device_id_type=MESH,
        )

    halo = [
        remote(vel_h.at[:, pl.ds(0, 2)], vb.at[:, pl.ds(BX + 2, 2), pl.ds(8, BY)], 0, left_x, gy),
        remote(vel_h.at[:, pl.ds(BX - 2, 2)], vb.at[:, pl.ds(0, 2), pl.ds(8, BY)], 1, right_x, gy),
        remote(ys.at[0], yr.at[1], 2, gx, left_y),
        remote(ys.at[1], yr.at[0], 3, gx, right_y),
    ]
    for n in (2, 3, 0, 1):
        halo[n].start()

    for i in range(1, GY):
        pl.semaphore_signal(all_sem, inc=1, device_id=(gx, lax.rem(gy + i, GY)), device_id_type=MESH)

    loads[1].wait()
    loads[2].wait()
    for full, high, low in ((vm_ref, vh, vl), (vt_ref, th, tl)):
        for i in range(0, NZ, 64):
            h, l = halves(full[i : i + 64, :])
            high[i : i + 64, :] = h
            low[i : i + 64, :] = l
    for n in range(6, 10):
        loads[n].wait()
    rate_row = jnp.concatenate([small[n : n + 1, :] for n in range(4)], axis=1)
    ie_ref[...] = 1.0 / (summed(narrow[2816:2944, :]) + rate_row)

    factor = small[4:5, 0:1]
    scale = factor * f32(-1.0 / 12.0)

    levels = lax.broadcasted_iota(jnp.int32, (BY, NZ), 1).astype(f32)
    diagonal = lax.broadcasted_iota(jnp.int32, (BY, BY), 0) == lax.broadcasted_iota(
        jnp.int32, (BY, BY), 1
    )

    def fluid_at(x):
        row = small[pl.ds(8 + x, 1), 0:BY]
        column = jnp.sum(jnp.where(diagonal, row, 0.0), axis=1, keepdims=True)
        return (levels >= column).astype(f32)

    def left_sides(group, field):
        for x in range(BX):
            f0 = field[0, x]
            if x:
                f0 = f0 - field[0, x - 1]
            f1 = field[1, x]
            lhs[group, BY * x : BY * x + BY, :] = f0 + (f1 - moved(f1, -1, 0))
            lhs[group, 144 + x : 145 + x, :] = -field[1, x, BY - 1 : BY, :]
        lhs[group, 128:144, :] = -field[0, BX - 1]
        lhs[group, 152:160, :] = jnp.zeros((8, NZ), f32)

    def forward(group, field):
        left_sides(group, field)
        wide_rows = dot3(halves(lhs[group]), (vh[...], vl[...]))
        tilted = dot3(halves(field[2].reshape(BX * BY, NZ)), (th[...], tl[...]))
        d = wide_rows[:128] + tilted
        d_parts = halves(d)
        p1 = dot3(unpacked(narrow, 0, 128, 128), d_parts)
        p1_ref[group] = p1
        w = halves(p1 * ie_ref[...])
        both = (
            jnp.concatenate([w[0], d_parts[0]], axis=0),
            jnp.concatenate([w[1], d_parts[1]], axis=0),
        )
        s = dot3(unpacked(mid, 1600, 64, 256), both)
        some, few = jnp.zeros((16, NZ), f32), jnp.zeros((8, NZ), f32)
        s = s + jnp.concatenate([some, wide_rows[128:144], few, wide_rows[144:152], some], axis=0)
        s = jnp.concatenate([s[:, : NZ // 2], s[:, NZ // 2 :]], axis=0)
        for i in range(2):
            sb[group, 128 * i : 128 * i + 128, :] = s[:, 128 * i : 128 * i + 128].T

    def chunk(n):
        return pl.ds(n * OWNED, OWNED)

    place = gy * GX + gx

    def to_owners(group):
        def copy_to(dx, dy):
            tx, ty = lax.rem(gx + dx, GX), lax.rem(half_y + dy, 8)
            return pltpu.make_async_remote_copy(
                src_ref=sb.at[group, chunk(tx * 8 + ty)], dst_ref=rbuf.at[chunk(place)],
                send_sem=a_send.at[group], recv_sem=a_recv.at[0],
                device_id=(tx, ty * 2 + group), device_id_type=MESH,
            )

        @pl.when(parity != group)
        def _():
            copy_to(0, 0).start()

        @pl.when(parity == group)
        def _():
            pltpu.make_async_copy(sb.at[group, chunk(owner)], rbuf.at[chunk(place)], a_recv.at[0]).start()

        def start(dx, carry):
            for dy in range(8):
                copy_to(dx, dy).start()
            return carry

        for dy in range(1, 8):
            copy_to(0, dy).start()
        lax.fori_loop(1, GX, start, 0)

    def span(ref, chunks, send, recv):
        rows = ref.at[pl.ds(0, chunks * OWNED)]
        return pltpu.make_async_remote_copy(
            src_ref=rows, dst_ref=rows, send_sem=a_send.at[send], recv_sem=a_recv.at[recv],
            device_id=(right_x, gy), device_id_type=MESH,
        )

    loads[3].wait()
    loads[10].wait()
    loads[11].wait()
    forward(1, cot)
    pl.semaphore_wait(all_sem, GY - 1)
    to_owners(1)

    loads[4].wait()
    halo[2].wait()
    halo[3].wait()
    for c in range(3):
        for x in range(BX):
            vb[c, x + 2, 6:8, :] = yr[0, c, 2 * x : 2 * x + 2, :]
            vb[c, x + 2, 8 + BY : 10 + BY, :] = yr[1, c, 2 * x : 2 * x + 2, :]

    def section_row(x, carry):
        fluid = fluid_at(x)
        kx, ky, kz = weights(adv[0, x]), weights(adv[1, x]), weights(adv[2, x])
        for c in range(3):
            center = vb[c, x + 2, 8 : 8 + BY, :]
            total = center * (kx[0] + ky[0] + kz[0])
            for offset in (-2, -1, 1, 2):
                total = total + kx[offset] * vb[c, x + 2 + offset, 8 : 8 + BY, :]
                total = total + ky[offset] * vb[c, x + 2, 8 + offset : 8 + BY + offset, :]
                total = total + kz[offset] * moved(center, offset, 1)
            sv[c, x] = fluid * (center + scale * total)
        return carry

    lax.fori_loop(2, BX - 2, section_row, 0)
    halo[0].wait()
    halo[1].wait()
    lax.fori_loop(0, 2, section_row, 0)
    lax.fori_loop(BX - 2, BX, section_row, 0)
    forward(0, sv)

    to_owners(0)

    loads[5].wait()
    span(rbuf, DEVICES, 0, 0).wait_recv()
    sides = [
        regroup([rbuf[32 * (8 * half + i) : 32 * (8 * half + i) + 32, :] for i in range(8)])
        for half in range(2)
    ]
    rows = [jnp.concatenate([sides[0][j], sides[1][j]], axis=1) for j in range(8)]
    along = dot3(halves(jnp.concatenate([rows[0], rows[4], rows[1], rows[5]], axis=0)), unpacked(mid, 512, 256, 256))
    columns = halves(jnp.concatenate([rows[2], rows[6]], axis=0))
    columns = dot(columns[0], mid[0:256, :]) + dot(columns[1], mid[0:256, :])
    for n in range(2):
        cs[n] = columns[:, 128 * n : 128 * n + 128]
    picked = [
        jnp.concatenate([cs[n, pl.ds(32 * half + m, GX, stride=OWNED), :] for n in range(2)], axis=1)
        for half in range(2)
        for m in range(OWNED)
    ]
    columns = halves(jnp.concatenate(regroup_wide(picked), axis=0))
    inner = dot3(unpacked(narrow, 2048, 64, 64), columns)
    inner = halves(jnp.concatenate([inner[:, 32 * n : 32 * n + 32] for n in range(8)], axis=0))
    along = halves(along)
    row_table, edge_table = unpacked(narrow, 256, 512, 128), unpacked(mid, 1536, 32, 256)
    left = [jnp.concatenate([row_table[i], inner[i]], axis=1) for i in range(2)]
    right = [jnp.concatenate([along[i], edge_table[i]], axis=0) for i in range(2)]
    hat = dot3(left, right)
    row = lax.broadcasted_iota(jnp.int32, (512, 128), 0)
    row_mode = lax.div(row, NX)
    rate = jnp.zeros((512, 128), f32)
    lane = lax.broadcasted_iota(jnp.int32, (1, 128), 1)
    first_lane = lax.rem(owner, 128 // OWNED) * OWNED
    for half in range(2):
        rates = small[pl.ds(2 * half + lax.div(owner, 128 // OWNED), 1), :]
        for m in range(OWNED):
            one = jnp.sum(jnp.where(lane == first_lane + m, rates, 0.0), axis=1, keepdims=True)
            rate = jnp.where(row_mode == OWNED * half + m, one, rate)
    lam_y = narrow[2944:2960, :].astype(f32)
    lam_y = [lam_y[n : n + 1] + (lam_y[n + 2 : n + 3] + lam_y[n + 4 : n + 5]) for n in range(2)]
    lam_y = jnp.concatenate(lam_y, axis=1)
    hat = halves(hat / (wide(rate + summed(narrow[2304:2816, :]), 256) + lam_y))
    along = dot3(halves(dot3(unpacked(large, 0, 128, 512), hat)), unpacked(mid, 1024, 256, 256))
    inner = dot3(hat, unpacked(narrow, 1536, 256, 32))
    inner = halves(jnp.concatenate([inner[NX * n : NX * n + NX] for n in range(8)], axis=1))
    columns = dot3(unpacked(narrow, 2176, 64, 64), inner)
    picked = regroup_wide([columns[8 * x : 8 * x + 8] for x in range(BX)])
    for half in range(2):
        for m in range(OWNED):
            for n in range(2):
                block = picked[OWNED * half + m][:, 128 * n : 128 * n + 128]
                cs[n, pl.ds(32 * half + m, GX, stride=OWNED), :] = block
    columns = halves(jnp.concatenate([cs[0], cs[1]], axis=1))
    columns = dot(columns[0], mid[256:512, :]) + dot(columns[1], mid[256:512, :])
    nothing = jnp.zeros((32, 256), f32)
    rows = [along[0:32], along[64:96], columns[0:32], nothing, along[32:64], along[96:128], columns[32:64], nothing]
    for half in range(2):
        for i, block in enumerate(regroup([r[:, 128 * half : 128 * half + 128] for r in rows])):
            ob[32 * (8 * half + i) : 32 * (8 * half + i) + 32, :] = block

    pltpu.make_async_copy(ob.at[chunk(place)], rb.at[parity, chunk(owner)], a_recv.at[1 + parity]).start()

    def answer(dx, dy):
        tx, ty = lax.rem(gx + dx, GX), lax.rem(gy + dy, GY)
        pltpu.make_async_remote_copy(
            src_ref=ob.at[chunk(ty * GX + tx)], dst_ref=rb.at[parity, chunk(owner)],
            send_sem=a_send.at[2], recv_sem=a_recv.at[1 + parity],
            device_id=(tx, ty), device_id_type=MESH,
        ).start()

    def answers(dx, carry):
        for dy in range(GY):
            answer(dx, dy)
        return carry

    for dy in range(1, GY):
        answer(0, dy)
    lax.fori_loop(1, GX, answers, 0)

    def backward(group):
        span(rb.at[group], OWNERS, 0, 1 + group).wait_recv()
        u = jnp.concatenate([rb[group, 0:128, :].T, rb[group, 128:256, :].T], axis=1)
        u = jnp.concatenate([u[0:SLOTS], u[SLOTS:]], axis=1)
        u_parts = halves(u)
        inside = (p1_ref[group] + dot3(unpacked(narrow, 1280, 128, 64), u_parts)) * ie_ref[...]
        in_parts = halves(inside)
        both = (
            jnp.concatenate([in_parts[0], u_parts[0]], axis=0),
            jnp.concatenate([in_parts[1], u_parts[1]], axis=0),
        )
        phi = dot3(unpacked(mid, 1728, 128, 192), both)
        ext = jnp.concatenate([phi, u[16:32], u[40:48], jnp.zeros((8, NZ), f32)], axis=0)
        lhs[group] = dot3(halves(ext), (vh[...], vl[...]), nt=True)
        return dot3(halves(phi), (th[...], tl[...]), nt=True)

    def corrections(group, x):
        here = lhs[group, BY * x : BY * x + BY, :]
        after = lhs[group, BY * x + BY : BY * x + 2 * BY, :]
        last = lax.broadcasted_iota(jnp.int32, (BY, NZ), 0) == BY - 1
        side = jnp.where(last, lhs[group, 144 + x : 145 + x, :], jnp.roll(here, -1, 0))
        return here - after, here - side

    tilted = backward(1)

    def gradient_row(x):
        fluid = fluid_at(x)
        c0, c1 = corrections(1, x)
        gp[0, x + 2] = fluid * (cot[0, x] - c0)
        gp[1, x + 2] = fluid * (cot[1, x] - c1)
        gp[2, x + 2] = fluid * (cot[2, x] - tilted[BY * x : BY * x + BY])
        sxp[x + 2] = adv[0, x]

    for x in (0, 1, BX - 2, BX - 1):
        gradient_row(x)

    k0, k1 = weights(adv[0, 0]), weights(adv[0, 1])
    k6, k7 = weights(adv[0, BX - 2]), weights(adv[0, BX - 1])
    for c in range(3):
        g0, g1, g6, g7 = gp[c, 2], gp[c, 3], gp[c, BX], gp[c, BX + 1]
        cxs[0, c, 0] = k0[-2] * g0
        cxs[0, c, 1] = k0[-1] * g0 + k1[-2] * g1
        cxs[1, c, 0] = k7[1] * g7 + k6[2] * g6
        cxs[1, c, 1] = k7[2] * g7
    edges = [
        remote(cxs.at[0], cxr.at[1], 4, left_x, gy),
        remote(cxs.at[1], cxr.at[0], 5, right_x, gy),
        remote(cys.at[0], cyr.at[1], 6, gx, left_y),
        remote(cys.at[1], cyr.at[0], 7, gx, right_y),
    ]
    edges[0].start()
    edges[1].start()
    for x in range(2, BX - 2):
        gradient_row(x)
    for x in range(BX):
        k = weights(adv[1, x])
        for c in range(3):
            g = gp[c, x + 2]
            one, two = k[-1] * g, k[-2] * g
            cys[0, c, 2 * x : 2 * x + 1, :] = two[0:1]
            cys[0, c, 2 * x + 1 : 2 * x + 2, :] = one[0:1] + two[1:2]
            one, two = k[1] * g, k[2] * g
            cys[1, c, 2 * x : 2 * x + 1, :] = one[BY - 1 : BY] + two[BY - 2 : BY - 1]
            cys[1, c, 2 * x + 1 : 2 * x + 2, :] = two[BY - 1 : BY]
    edges[2].start()
    edges[3].start()
    nothing = jnp.zeros((2, BY, NZ), f32)
    for c in range(3):
        gp[c, 0:2] = nothing
        gp[c, BX + 2 : BX + 4] = nothing
    sxp[0:2] = nothing
    sxp[BX + 2 : BX + 4] = nothing

    def adjoint_row(x, carry):
        kx = {}
        for offset in (-2, -1, 0, 1, 2):
            kx[offset] = weights(sxp[x + 2 - offset])[offset]
        ky, kz = weights(adv[1, x]), weights(adv[2, x])
        for c in range(3):
            center = gp[c, x + 2]
            total = center * (kx[0] + ky[0] + kz[0])
            for offset in (-2, -1, 1, 2):
                total = total + kx[offset] * gp[c, x + 2 - offset]
                total = total + moved(ky[offset] * center, -offset, 0)
                total = total + moved(kz[offset] * center, -offset, 1)
            adj_ref[c, x] = center + scale * total
        return carry

    lax.fori_loop(0, BX, adjoint_row, 0)

    tilted = backward(0)
    for x in range(BX):
        c0, c1 = corrections(0, x)
        next_ref[0, x] = sv[0, x] - c0
        next_ref[1, x] = sv[1, x] - c1
        next_ref[2, x] = sv[2, x] - tilted[BY * x : BY * x + BY]

    for copy in edges:
        copy.wait()
    for c in range(3):
        for n in range(2):
            adj_ref[c, n] += scale * cxr[0, c, n]
            adj_ref[c, BX - 2 + n] += scale * cxr[1, c, n]
        for x in range(BX):
            adj_ref[c, x, 0:2, :] += scale * cyr[0, c, 2 * x : 2 * x + 2, :]
            adj_ref[c, x, BY - 2 : BY, :] += scale * cyr[1, c, 2 * x : 2 * x + 2, :]

    span(rbuf, DEVICES - 1, 2, 0).wait_send()
    for group in range(2):

        @pl.when(parity != group)
        def _():
            span(rbuf, OWNERS, group, 0).wait_send()

        @pl.when(parity == group)
        def _():
            span(rbuf, OWNERS - 1, group, 0).wait_send()


def write_out(next_ref, adj_ref, next_out, adj_out, sems):
    copies = [
        pltpu.make_async_copy(next_ref, next_out, sems.at[0]),
        pltpu.make_async_copy(adj_ref, adj_out, sems.at[1]),
    ]
    for copy in copies:
        copy.start()
    for copy in copies:
        copy.wait()


def section_factor(section_index):
    section = lax.rem(section_index[0], 3)
    step = lax.div(section_index[0], 3).astype(f32)
    size = f32(0.2) + f32(0.2) * step / f32(63.0)
    return size * jnp.where(section == 0, f32(1.0 / 3.0), jnp.where(section == 1, f32(0.5), f32(1.0)))


def per_device(
    velocity_now, advecting, cotangent, building_height, section_index,
    vertical_modes, vertical_tilt, mode_rates,
):
    small = jnp.concatenate(
        [
            mode_rates.reshape(4, 128),
            jnp.broadcast_to(section_factor(section_index), (4, 128)),
            jnp.pad(building_height, ((0, 0), (0, 128 - BY))).astype(f32),
        ]
    )
    vmem = pl.BlockSpec(memory_space=pltpu.VMEM)
    hbm = pl.BlockSpec(memory_space=pltpu.HBM)
    field = jax.ShapeDtypeStruct((3, BX, BY, NZ), f32)
    results = pl.pallas_call(
        kernel,
        out_shape=(field, field),
        in_specs=[hbm, hbm, hbm, vmem, hbm, hbm, hbm],
        out_specs=(vmem, vmem),
        scratch_shapes=[
            pltpu.VMEM((3, BX + 4, 32, NZ), f32),
            pltpu.VMEM((3, BX, BY, NZ), f32),
            pltpu.VMEM((3, BX, BY, NZ), f32),
            pltpu.VMEM((NZ, NZ), f32),
            pltpu.VMEM((NZ, NZ), f32),
            pltpu.VMEM((LARGE, 512), bf16),
            pltpu.VMEM((2 * MID, 256), bf16),
            pltpu.VMEM((4 * NARROW, 128), bf16),
            pltpu.VMEM((3, BX, BY, NZ), f32),
            pltpu.VMEM((2, 160, NZ), f32),
            pltpu.VMEM((NZ, NZ), bf16),
            pltpu.VMEM((NZ, NZ), bf16),
            pltpu.VMEM((NZ, NZ), bf16),
            pltpu.VMEM((NZ, NZ), bf16),
            pltpu.VMEM((2, 3, 16, NZ), f32),
            pltpu.VMEM((2, 3, 16, NZ), f32),
            pltpu.VMEM((2, NZ // 2, 128), f32),
            pltpu.VMEM((NZ, 128), f32),
            pltpu.VMEM((NZ, 128), f32),
            pltpu.VMEM((2, NZ // 2, 128), f32),
            pltpu.VMEM((3, BX + 4, BY, NZ), f32),
            pltpu.VMEM((BX + 4, BY, NZ), f32),
            pltpu.VMEM((2, 3, 2, BY, NZ), f32),
            pltpu.VMEM((2, 3, 2, BY, NZ), f32),
            pltpu.VMEM((2, 3, 16, NZ), f32),
            pltpu.VMEM((2, 3, 16, NZ), f32),
            pltpu.VMEM((2, 128, NZ), f32),
            pltpu.VMEM((128, NZ), f32),
            pltpu.VMEM((2, 64, 128), f32),
            pltpu.SemaphoreType.DMA((3,)),
            pltpu.SemaphoreType.DMA((3,)),
            pltpu.SemaphoreType.DMA((8,)),
            pltpu.SemaphoreType.DMA((8,)),
            pltpu.SemaphoreType.DMA((12,)),
            pltpu.SemaphoreType.REGULAR,
        ],
        compiler_params=pltpu.CompilerParams(
            collective_id=0, has_side_effects=True, vmem_limit_bytes=52 * 1024 * 1024
        ),
    )(
        velocity_now, advecting, cotangent, small, vertical_modes, vertical_tilt, tables(),
    )
    return pl.pallas_call(
        write_out,
        out_shape=(field, field),
        in_specs=[vmem, vmem],
        out_specs=(hbm, hbm),
        scratch_shapes=[pltpu.SemaphoreType.DMA((2,))],
        compiler_params=pltpu.CompilerParams(vmem_limit_bytes=8 * 1024 * 1024),
    )(*results)


def solution(mesh):
    blocks = P(None, "gx", "gy", None)
    return jax.shard_map(
        per_device,
        mesh=mesh,
        in_specs=(blocks, blocks, blocks, P("gx", "gy"), P(), P(), P(), P()),
        out_specs=(blocks, blocks),
        check_vma=False,
    )
```

```python
import functools
import math

import jax
import jax.numpy as jnp
import ml_dtypes
import numpy as np
from jax import lax
from jax.experimental import pallas as pl
from jax.experimental.pallas import tpu as pltpu
from jax.sharding import PartitionSpec as P

MESH = pl.DeviceIdType.MESH
BX, BY = 8, 16
GX, GY = 8, 16
NX, NY, NZ = 64, 256, 512
DEVICES = GX * GY
OWNERS = DEVICES // 2
OWNED = NZ // OWNERS // 2
SLOTS = 64
LARGE, MID, NARROW = 256, 992, 752
f32, bf16 = jnp.float32, jnp.bfloat16


def fourier(n):
    place = np.arange(n)
    basis = np.zeros((n, n))
    freq = np.zeros(n)
    for column in range(n):
        k = (column + 1) // 2
        angle = 2.0 * math.pi * k * place / n
        if column == 0 or k == n // 2:
            basis[:, column] = np.cos(angle) / math.sqrt(n)
        else:
            basis[:, column] = (np.cos(angle) if column % 2 else np.sin(angle)) * math.sqrt(2.0 / n)
        freq[column] = 2.0 - 2.0 * math.cos(2.0 * math.pi * k / n)
    return basis, freq


def split_const(matrix, count=2):
    parts = []
    for _ in range(count):
        parts.append(matrix.astype(ml_dtypes.bfloat16))
        matrix = matrix - parts[-1].astype(np.float64)
    return parts


def tables():
    j, k = np.arange(BX), np.arange(BY)
    sin_x = math.sqrt(2.0 / BX) * np.sin(math.pi * np.outer(j, j) / BX)
    sin_y = math.sqrt(2.0 / BY) * np.sin(math.pi * np.outer(k, k) / BY)
    sin_x[0], sin_x[:, 0], sin_y[0], sin_y[:, 0] = 0.0, 0.0, 0.0, 0.0
    sine = np.kron(sin_x, sin_y)
    mu = (2.0 - 2.0 * np.cos(math.pi * j / BX))[:, None] + (2.0 - 2.0 * np.cos(math.pi * k / BY))
    near = np.zeros((SLOTS, BX * BY))
    own = np.zeros((SLOTS, BX * BY))
    for y in range(BY):
        own[y, y] = 1.0
        if y:
            near[y] = sine[1 * BY + y]
            near[16 + y] = sine[(BX - 1) * BY + y]
    for x in range(1, BX):
        own[32 + x, x * BY] = 1.0
        near[32 + x] = sine[x * BY + 1]
        near[40 + x] = sine[x * BY + BY - 1]
    to_slots = np.concatenate([near, own], 1)
    from_slots = np.concatenate([sine, own.T], 1)
    qx, lx = fourier(NX)
    qy, ly = fourier(NY)
    order = np.zeros((GY, 2, BX, BX, 2, GY))
    for g in range(GY):
        for kind in range(2):
            for x in range(BX):
                order[g, kind, x, x, kind, g] = 1.0
    order = order.reshape(256, 256)
    rows = np.zeros((2, OWNED, NX, 2, 2, GX, OWNED))
    for group in range(2):
        for mode in range(OWNED):
            for g in range(GX):
                for kind in range(2):
                    rows[group, mode, :, kind, group, g, mode] = qx[8 * (g + kind) % NX]
    rows = rows.reshape(512, 128)
    cols = qx.reshape(GX, BX, NX).transpose(2, 1, 0).reshape(NX, NX)
    wc = np.stack([qy[0::16], np.roll(qy[0::16], -1, axis=0)]).reshape(32, 256)
    lam_x = np.tile(lx, 2 * OWNED)

    def columns(values):
        out = np.zeros((values.size, 128), ml_dtypes.bfloat16)
        for n, part in enumerate(split_const(values.reshape(-1), 3)):
            out[:, n] = part
        return out

    def packed(matrices, lanes):
        parts = []
        for matrix in matrices:
            for part in split_const(np.ascontiguousarray(matrix)):
                parts.append(np.pad(part, ((0, 0), (0, lanes - part.shape[1]))))
        return np.concatenate(parts)

    exact = np.concatenate([order, order.T]).astype(ml_dtypes.bfloat16)
    lam_y = np.stack(split_const(ly, 3)).reshape(6, 128)
    large = packed([rows.T], 512)
    mid = np.concatenate([exact, packed([qy, qy.T, wc, to_slots, from_slots], 256)])
    narrow = np.concatenate([packed([sine, rows, near.T, wc.T, cols, cols.T], 128), columns(lam_x), columns(mu), lam_y])
    narrow = np.pad(narrow, ((0, 4 * NARROW - narrow.shape[0]), (0, 0)))
    mid = np.concatenate([mid[:MID], mid[MID:]], axis=1)
    narrow = np.concatenate([narrow[NARROW * i : NARROW * i + NARROW] for i in range(4)], axis=1)
    return jnp.asarray(np.concatenate([large, mid, narrow]))


def summed(parts):
    parts = parts.astype(f32)
    return parts[:, 0:1] + (parts[:, 1:2] + parts[:, 2:3])


def unpacked(ref, start, rows, lanes):
    return ref[start : start + rows, :lanes], ref[start + rows : start + 2 * rows, :lanes]


def halves(value):
    high = value.astype(bf16)
    low = (value - high.astype(f32)).astype(bf16)
    return high, low


def dot(a, b, nt=False):
    dims = (((1,), (1 if nt else 0,)), ((), ()))
    return lax.dot_general(a, b, dims, preferred_element_type=f32)


def regroup(blocks):
    blocks = list(blocks)
    lanes = 128 // len(blocks)
    group = lax.broadcasted_iota(jnp.int32, blocks[0].shape, 1) // lanes
    step = len(blocks) // 2
    while step:
        low = (group & step) == 0
        for i in range(len(blocks)):
            if not i & step:
                a, b = blocks[i], blocks[i + step]
                blocks[i] = jnp.where(low, a, pltpu.roll(b, lanes * step, 1))
                blocks[i + step] = jnp.where(low, pltpu.roll(a, 128 - lanes * step, 1), b)
        step //= 2
    return blocks


def regroup_wide(blocks):
    out = []
    for right in range(2):
        quads = [regroup([b[:, 128 * right : 128 * right + 128] for b in blocks[4 * n : 4 * n + 4]]) for n in range(2)]
        out.extend(jnp.concatenate([a, b], axis=1) for a, b in zip(*quads))
    return out


def dot3(a, b, nt=False):
    n = a[0].shape[0]
    both = dot(jnp.concatenate([a[0], a[1]], axis=0), b[0], nt)
    return both[:n] + (dot(a[0], b[1], nt) + both[n:])


def wide(column, lanes):
    return jnp.concatenate([column] * (lanes // 128), axis=1)


TAPS = ((-2, 1.0, 1.0), (-1, -8.0, -4.0), (0, 0.0, 6.0), (1, 8.0, -4.0), (2, -1.0, 1.0))


def weights(speed):
    size = jnp.abs(speed)
    out = {}
    for offset, central, hyper in TAPS:
        out[offset] = hyper * size + central * speed if central else hyper * size
    return out


def moved(value, offset, axis):
    n = value.shape[axis]
    if axis == 1:
        rolled = pltpu.roll(value, (-offset) % n, 1)
    else:
        rolled = jnp.roll(value, -offset, 0)
    place = lax.broadcasted_iota(jnp.int32, value.shape, axis)
    keep = place < n - offset if offset > 0 else place >= -offset
    return jnp.where(keep, rolled, 0.0)


def kernel(
    vel_h, adv_h, cot_h, small, vm_h, vt_h, tables_h,
    next_ref, adj_ref,
    vb, adv, cot, vm_ref, vt_ref, large, mid, narrow,
    sv, lhs, vh, vl, th, tl, ys, yr, sb, rbuf, ob, rb, gp, sxp, cxs, cxr, cys, cyr,
    p1_ref, ie_ref, cs,
    a_send, a_recv, h_send, h_recv, l_sem, all_sem,
):
    gx, gy = lax.axis_index("gx"), lax.axis_index("gy")
    me = gx * GY + gy
    left_x, right_x = lax.rem(gx + GX - 1, GX), lax.rem(gx + 1, GX)
    left_y, right_y = lax.rem(gy + GY - 1, GY), lax.rem(gy + 1, GY)

    parity, half_y = lax.rem(gy, 2), lax.div(gy, 2)
    owner = gx * 8 + half_y
    barrier = pltpu.get_barrier_semaphore()
    for i in range(1, GX):
        pl.semaphore_signal(barrier, inc=1, device_id=(lax.rem(gx + i, GX), gy), device_id_type=MESH)
    for i in range(1, GY):
        pl.semaphore_signal(barrier, inc=1, device_id=(gx, lax.rem(gy + i, GY)), device_id_type=MESH)

    loads = [
        pltpu.make_async_copy(source, target, l_sem.at[n])
        for n, (source, target) in enumerate(
            (
                (vel_h, vb.at[:, pl.ds(2, BX), pl.ds(8, BY)]),
                (vm_h, vm_ref),
                (vt_h, vt_ref),
                (cot_h, cot),
                (adv_h, adv),
                (tables_h.at[pl.ds(0, LARGE)], large),
            )
            + tuple(
                (tables_h.at[pl.ds(LARGE + MID, NARROW), pl.ds(128 * i, 128)], narrow.at[pl.ds(NARROW * i, NARROW)])
                for i in range(4)
            )
            + tuple(
                (tables_h.at[pl.ds(LARGE, MID), pl.ds(256 * i, 256)], mid.at[pl.ds(MID * i, MID)])
                for i in range(2)
            )
        )
    ]
    for n in (0, 3, 1, 2, 6, 7, 8, 9, 10, 11, 4, 5):
        loads[n].start()
    pl.semaphore_wait(barrier, GX + GY - 2)

    def remote(src, dst, n, x, y):
        return pltpu.make_async_remote_copy(
            src_ref=src, dst_ref=dst, send_sem=h_send.at[n], recv_sem=h_recv.at[n],
            device_id=(x, y), device_id_type=MESH,
        )

    halo = [
        remote(vel_h.at[:, pl.ds(0, 2)], vb.at[:, pl.ds(BX + 2, 2), pl.ds(8, BY)], 0, left_x, gy),
        remote(vel_h.at[:, pl.ds(BX - 2, 2)], vb.at[:, pl.ds(0, 2), pl.ds(8, BY)], 1, right_x, gy),
        remote(ys.at[0], yr.at[1], 2, gx, left_y),
        remote(ys.at[1], yr.at[0], 3, gx, right_y),
    ]

    for i in range(1, GY):
        pl.semaphore_signal(all_sem, inc=1, device_id=(gx, lax.rem(gy + i, GY)), device_id_type=MESH)

    loads[0].wait()

    for c in range(3):
        for x in range(BX):
            ys[0, c, 2 * x : 2 * x + 2, :] = vb[c, x + 2, 8:10, :]
            ys[1, c, 2 * x : 2 * x + 2, :] = vb[c, x + 2, 6 + BY : 8 + BY, :]
    halo[2].start()
    halo[3].start()

    loads[1].wait()
    loads[2].wait()
    for full, high, low in ((vm_ref, vh, vl), (vt_ref, th, tl)):
        for i in range(0, NZ, 64):
            h, l = halves(full[i : i + 64, :])
            high[i : i + 64, :] = h
            low[i : i + 64, :] = l
    for n in range(6, 10):
        loads[n].wait()
    rate_row = jnp.concatenate([small[n : n + 1, :] for n in range(4)], axis=1)
    ie_ref[...] = 1.0 / (summed(narrow[2816:2944, :]) + rate_row)

    factor = small[4:5, 0:1]
    scale = factor * f32(-1.0 / 12.0)

    levels = lax.broadcasted_iota(jnp.int32, (BY, NZ), 1).astype(f32)
    diagonal = lax.broadcasted_iota(jnp.int32, (BY, BY), 0) == lax.broadcasted_iota(
        jnp.int32, (BY, BY), 1
    )

    def fluid_at(x):
        row = small[pl.ds(8 + x, 1), 0:BY]
        column = jnp.sum(jnp.where(diagonal, row, 0.0), axis=1, keepdims=True)
        return (levels >= column).astype(f32)

    def left_sides(group, field):
        for x in range(BX):
            f0 = field[0, x]
            if x:
                f0 = f0 - field[0, x - 1]
            f1 = field[1, x]
            lhs[group, BY * x : BY * x + BY, :] = f0 + (f1 - moved(f1, -1, 0))
            lhs[group, 144 + x : 145 + x, :] = -field[1, x, BY - 1 : BY, :]
        lhs[group, 128:144, :] = -field[0, BX - 1]
        lhs[group, 152:160, :] = jnp.zeros((8, NZ), f32)

    def forward(group, field):
        left_sides(group, field)
        wide_rows = dot3(halves(lhs[group]), (vh[...], vl[...]))
        tilted = dot3(halves(field[2].reshape(BX * BY, NZ)), (th[...], tl[...]))
        d = wide_rows[:128] + tilted
        d_parts = halves(d)
        p1 = dot3(unpacked(narrow, 0, 128, 128), d_parts)
        p1_ref[group] = p1
        w = halves(p1 * ie_ref[...])
        both = (
            jnp.concatenate([w[0], d_parts[0]], axis=0),
            jnp.concatenate([w[1], d_parts[1]], axis=0),
        )
        s = dot3(unpacked(mid, 1600, 64, 256), both)
        some, few = jnp.zeros((16, NZ), f32), jnp.zeros((8, NZ), f32)
        s = s + jnp.concatenate([some, wide_rows[128:144], few, wide_rows[144:152], some], axis=0)
        s = jnp.concatenate([s[:, : NZ // 2], s[:, NZ // 2 :]], axis=0)
        for i in range(2):
            sb[group, 128 * i : 128 * i + 128, :] = s[:, 128 * i : 128 * i + 128].T

    def chunk(n):
        return pl.ds(n * OWNED, OWNED)

    place = gy * GX + gx

    def to_owners(group):
        def copy_to(dx, dy):
            tx, ty = lax.rem(gx + dx, GX), lax.rem(half_y + dy, 8)
            return pltpu.make_async_remote_copy(
                src_ref=sb.at[group, chunk(tx * 8 + ty)], dst_ref=rbuf.at[chunk(place)],
                send_sem=a_send.at[group], recv_sem=a_recv.at[0],
                device_id=(tx, ty * 2 + group), device_id_type=MESH,
            )

        @pl.when(parity != group)
        def _():
            copy_to(0, 0).start()

        @pl.when(parity == group)
        def _():
            pltpu.make_async_copy(sb.at[group, chunk(owner)], rbuf.at[chunk(place)], a_recv.at[0]).start()

        def start(dx, carry):
            for dy in range(8):
                copy_to(dx, dy).start()
            return carry

        for dy in range(1, 8):
            copy_to(0, dy).start()
        lax.fori_loop(1, GX, start, 0)

    def span(ref, chunks, send, recv):
        rows = ref.at[pl.ds(0, chunks * OWNED)]
        return pltpu.make_async_remote_copy(
            src_ref=rows, dst_ref=rows, send_sem=a_send.at[send], recv_sem=a_recv.at[recv],
            device_id=(right_x, gy), device_id_type=MESH,
        )

    loads[3].wait()
    loads[10].wait()
    loads[11].wait()
    forward(1, cot)
    pl.semaphore_wait(all_sem, GY - 1)
    to_owners(1)
    halo[0].start()
    halo[1].start()

    loads[4].wait()
    def own():
        loads[5].wait()
        span(rbuf, DEVICES, 0, 0).wait_recv()
        sides = [
            regroup([rbuf[32 * (8 * half + i) : 32 * (8 * half + i) + 32, :] for i in range(8)])
            for half in range(2)
        ]
        rows = [jnp.concatenate([sides[0][j], sides[1][j]], axis=1) for j in range(8)]
        along = dot3(halves(jnp.concatenate([rows[0], rows[4], rows[1], rows[5]], axis=0)), unpacked(mid, 512, 256, 256))
        columns = halves(jnp.concatenate([rows[2], rows[6]], axis=0))
        columns = dot(columns[0], mid[0:256, :]) + dot(columns[1], mid[0:256, :])
        for n in range(2):
            cs[n] = columns[:, 128 * n : 128 * n + 128]
        picked = [
            jnp.concatenate([cs[n, pl.ds(32 * half + m, GX, stride=OWNED), :] for n in range(2)], axis=1)
            for half in range(2)
            for m in range(OWNED)
        ]
        columns = halves(jnp.concatenate(regroup_wide(picked), axis=0))
        inner = dot3(unpacked(narrow, 2048, 64, 64), columns)
        inner = halves(jnp.concatenate([inner[:, 32 * n : 32 * n + 32] for n in range(8)], axis=0))
        along = halves(along)
        row_table, edge_table = unpacked(narrow, 256, 512, 128), unpacked(mid, 1536, 32, 256)
        left = [jnp.concatenate([row_table[i], inner[i]], axis=1) for i in range(2)]
        right = [jnp.concatenate([along[i], edge_table[i]], axis=0) for i in range(2)]
        hat = dot3(left, right)
        row = lax.broadcasted_iota(jnp.int32, (512, 128), 0)
        row_mode = lax.div(row, NX)
        rate = jnp.zeros((512, 128), f32)
        lane = lax.broadcasted_iota(jnp.int32, (1, 128), 1)
        first_lane = lax.rem(owner, 128 // OWNED) * OWNED
        for half in range(2):
            rates = small[pl.ds(2 * half + lax.div(owner, 128 // OWNED), 1), :]
            for m in range(OWNED):
                one = jnp.sum(jnp.where(lane == first_lane + m, rates, 0.0), axis=1, keepdims=True)
                rate = jnp.where(row_mode == OWNED * half + m, one, rate)
        lam_y = narrow[2944:2960, :].astype(f32)
        lam_y = [lam_y[n : n + 1] + (lam_y[n + 2 : n + 3] + lam_y[n + 4 : n + 5]) for n in range(2)]
        lam_y = jnp.concatenate(lam_y, axis=1)
        hat = halves(hat / (wide(rate + summed(narrow[2304:2816, :]), 256) + lam_y))
        along = dot3(halves(dot3(unpacked(large, 0, 128, 512), hat)), unpacked(mid, 1024, 256, 256))
        inner = dot3(hat, unpacked(narrow, 1536, 256, 32))
        inner = halves(jnp.concatenate([inner[NX * n : NX * n + NX] for n in range(8)], axis=1))
        columns = dot3(unpacked(narrow, 2176, 64, 64), inner)
        picked = regroup_wide([columns[8 * x : 8 * x + 8] for x in range(BX)])
        for half in range(2):
            for m in range(OWNED):
                for n in range(2):
                    block = picked[OWNED * half + m][:, 128 * n : 128 * n + 128]
                    cs[n, pl.ds(32 * half + m, GX, stride=OWNED), :] = block
        columns = halves(jnp.concatenate([cs[0], cs[1]], axis=1))
        columns = dot(columns[0], mid[256:512, :]) + dot(columns[1], mid[256:512, :])
        nothing = jnp.zeros((32, 256), f32)
        rows = [along[0:32], along[64:96], columns[0:32], nothing, along[32:64], along[96:128], columns[32:64], nothing]
        for half in range(2):
            for i, block in enumerate(regroup([r[:, 128 * half : 128 * half + 128] for r in rows])):
                ob[32 * (8 * half + i) : 32 * (8 * half + i) + 32, :] = block

        pltpu.make_async_copy(ob.at[chunk(place)], rb.at[parity, chunk(owner)], a_recv.at[1 + parity]).start()

        def answer(dx, dy):
            tx, ty = lax.rem(gx + dx, GX), lax.rem(gy + dy, GY)
            pltpu.make_async_remote_copy(
                src_ref=ob.at[chunk(ty * GX + tx)], dst_ref=rb.at[parity, chunk(owner)],
                send_sem=a_send.at[2], recv_sem=a_recv.at[1 + parity],
                device_id=(tx, ty), device_id_type=MESH,
            ).start()

        def answers(dx, carry):
            for dy in range(GY):
                answer(dx, dy)
            return carry

        for dy in range(1, GY):
            answer(0, dy)
        lax.fori_loop(1, GX, answers, 0)

    halo[2].wait()
    halo[3].wait()
    for c in range(3):
        for x in range(BX):
            vb[c, x + 2, 6:8, :] = yr[0, c, 2 * x : 2 * x + 2, :]
            vb[c, x + 2, 8 + BY : 10 + BY, :] = yr[1, c, 2 * x : 2 * x + 2, :]

    def section_row(x, carry):
        fluid = fluid_at(x)
        kx, ky, kz = weights(adv[0, x]), weights(adv[1, x]), weights(adv[2, x])
        for c in range(3):
            center = vb[c, x + 2, 8 : 8 + BY, :]
            total = center * (kx[0] + ky[0] + kz[0])
            for offset in (-2, -1, 1, 2):
                total = total + kx[offset] * vb[c, x + 2 + offset, 8 : 8 + BY, :]
                total = total + ky[offset] * vb[c, x + 2, 8 + offset : 8 + BY + offset, :]
                total = total + kz[offset] * moved(center, offset, 1)
            sv[c, x] = fluid * (center + scale * total)
        return carry

    lax.fori_loop(2, BX - 2, section_row, 0)
    pl.when(parity == 1)(own)
    halo[0].wait()
    halo[1].wait()
    lax.fori_loop(0, 2, section_row, 0)
    lax.fori_loop(BX - 2, BX, section_row, 0)
    forward(0, sv)

    to_owners(0)

    def backward(group):
        span(rb.at[group], OWNERS, 0, 1 + group).wait_recv()
        u = jnp.concatenate([rb[group, 0:128, :].T, rb[group, 128:256, :].T], axis=1)
        u = jnp.concatenate([u[0:SLOTS], u[SLOTS:]], axis=1)
        u_parts = halves(u)
        inside = (p1_ref[group] + dot3(unpacked(narrow, 1280, 128, 64), u_parts)) * ie_ref[...]
        in_parts = halves(inside)
        both = (
            jnp.concatenate([in_parts[0], u_parts[0]], axis=0),
            jnp.concatenate([in_parts[1], u_parts[1]], axis=0),
        )
        phi = dot3(unpacked(mid, 1728, 128, 192), both)
        ext = jnp.concatenate([phi, u[16:32], u[40:48], jnp.zeros((8, NZ), f32)], axis=0)
        lhs[group] = dot3(halves(ext), (vh[...], vl[...]), nt=True)
        return halves(phi)

    def tilt(phi):
        return dot3(phi, (th[...], tl[...]), nt=True)

    def corrections(group, x):
        here = lhs[group, BY * x : BY * x + BY, :]
        after = lhs[group, BY * x + BY : BY * x + 2 * BY, :]
        last = lax.broadcasted_iota(jnp.int32, (BY, NZ), 0) == BY - 1
        side = jnp.where(last, lhs[group, 144 + x : 145 + x, :], jnp.roll(here, -1, 0))
        return here - after, here - side

    phi = backward(1)

    def gradient_row(x):
        fluid = fluid_at(x)
        c0, c1 = corrections(1, x)
        gp[0, x + 2] = fluid * (cot[0, x] - c0)
        gp[1, x + 2] = fluid * (cot[1, x] - c1)
        sxp[x + 2] = adv[0, x]

    def gradient_row_z(x):
        gp[2, x + 2] = fluid_at(x) * (cot[2, x] - tilted[BY * x : BY * x + BY])

    for x in (0, 1, BX - 2, BX - 1):
        gradient_row(x)

    k0, k1 = weights(adv[0, 0]), weights(adv[0, 1])
    k6, k7 = weights(adv[0, BX - 2]), weights(adv[0, BX - 1])
    edges = [
        remote(cxs.at[0, pl.ds(0, 2)], cxr.at[1, pl.ds(0, 2)], 4, left_x, gy),
        remote(cxs.at[1, pl.ds(0, 2)], cxr.at[0, pl.ds(0, 2)], 5, right_x, gy),
        remote(cys.at[0], cyr.at[1], 6, gx, left_y),
        remote(cys.at[1], cyr.at[0], 7, gx, right_y),
        remote(cxs.at[0, pl.ds(2, 1)], cxr.at[1, pl.ds(2, 1)], 8, left_x, gy),
        remote(cxs.at[1, pl.ds(2, 1)], cxr.at[0, pl.ds(2, 1)], 9, right_x, gy),
    ]

    def contributions_x(c):
        g0, g1, g6, g7 = gp[c, 2], gp[c, 3], gp[c, BX], gp[c, BX + 1]
        cxs[0, c, 0] = k0[-2] * g0
        cxs[0, c, 1] = k0[-1] * g0 + k1[-2] * g1
        cxs[1, c, 0] = k7[1] * g7 + k6[2] * g6
        cxs[1, c, 1] = k7[2] * g7

    contributions_x(0)
    contributions_x(1)
    edges[0].start()
    edges[1].start()
    tilted = tilt(phi)
    for x in (0, 1, BX - 2, BX - 1):
        gradient_row_z(x)
    contributions_x(2)
    edges[4].start()
    edges[5].start()
    for x in range(2, BX - 2):
        gradient_row(x)
        gradient_row_z(x)
    for x in range(BX):
        k = weights(adv[1, x])
        for c in range(3):
            g = gp[c, x + 2]
            one, two = k[-1] * g, k[-2] * g
            cys[0, c, 2 * x : 2 * x + 1, :] = two[0:1]
            cys[0, c, 2 * x + 1 : 2 * x + 2, :] = one[0:1] + two[1:2]
            one, two = k[1] * g, k[2] * g
            cys[1, c, 2 * x : 2 * x + 1, :] = one[BY - 1 : BY] + two[BY - 2 : BY - 1]
            cys[1, c, 2 * x + 1 : 2 * x + 2, :] = two[BY - 1 : BY]
    edges[2].start()
    edges[3].start()
    pl.when(parity == 0)(own)
    nothing = jnp.zeros((2, BY, NZ), f32)
    for c in range(3):
        gp[c, 0:2] = nothing
        gp[c, BX + 2 : BX + 4] = nothing
    sxp[0:2] = nothing
    sxp[BX + 2 : BX + 4] = nothing

    def adjoint_row(x, carry):
        kx = {}
        for offset in (-2, -1, 0, 1, 2):
            kx[offset] = weights(sxp[x + 2 - offset])[offset]
        ky, kz = weights(adv[1, x]), weights(adv[2, x])
        for c in range(3):
            center = gp[c, x + 2]
            total = center * (kx[0] + ky[0] + kz[0])
            for offset in (-2, -1, 1, 2):
                total = total + kx[offset] * gp[c, x + 2 - offset]
                total = total + moved(ky[offset] * center, -offset, 0)
                total = total + moved(kz[offset] * center, -offset, 1)
            adj_ref[c, x] = center + scale * total
        return carry

    lax.fori_loop(0, BX, adjoint_row, 0)

    tilted = tilt(backward(0))
    for x in range(BX):
        c0, c1 = corrections(0, x)
        next_ref[0, x] = sv[0, x] - c0
        next_ref[1, x] = sv[1, x] - c1
        next_ref[2, x] = sv[2, x] - tilted[BY * x : BY * x + BY]

    for copy in edges:
        copy.wait()
    for c in range(3):
        for n in range(2):
            adj_ref[c, n] += scale * cxr[0, c, n]
            adj_ref[c, BX - 2 + n] += scale * cxr[1, c, n]
        for x in range(BX):
            adj_ref[c, x, 0:2, :] += scale * cyr[0, c, 2 * x : 2 * x + 2, :]
            adj_ref[c, x, BY - 2 : BY, :] += scale * cyr[1, c, 2 * x : 2 * x + 2, :]

    span(rbuf, DEVICES - 1, 2, 0).wait_send()
    for group in range(2):

        @pl.when(parity != group)
        def _():
            span(rbuf, OWNERS, group, 0).wait_send()

        @pl.when(parity == group)
        def _():
            span(rbuf, OWNERS - 1, group, 0).wait_send()


def write_out(next_ref, adj_ref, next_out, adj_out, sems):
    copies = [
        pltpu.make_async_copy(next_ref, next_out, sems.at[0]),
        pltpu.make_async_copy(adj_ref, adj_out, sems.at[1]),
    ]
    for copy in copies:
        copy.start()
    for copy in copies:
        copy.wait()


def section_factor(section_index):
    section = lax.rem(section_index[0], 3)
    step = lax.div(section_index[0], 3).astype(f32)
    size = f32(0.2) + f32(0.2) * step / f32(63.0)
    return size * jnp.where(section == 0, f32(1.0 / 3.0), jnp.where(section == 1, f32(0.5), f32(1.0)))


def per_device(
    velocity_now, advecting, cotangent, building_height, section_index,
    vertical_modes, vertical_tilt, mode_rates,
):
    small = jnp.concatenate(
        [
            mode_rates.reshape(4, 128),
            jnp.broadcast_to(section_factor(section_index), (4, 128)),
            jnp.pad(building_height, ((0, 0), (0, 128 - BY))).astype(f32),
        ]
    )
    vmem = pl.BlockSpec(memory_space=pltpu.VMEM)
    hbm = pl.BlockSpec(memory_space=pltpu.HBM)
    field = jax.ShapeDtypeStruct((3, BX, BY, NZ), f32)
    results = pl.pallas_call(
        kernel,
        out_shape=(field, field),
        in_specs=[hbm, hbm, hbm, vmem, hbm, hbm, hbm],
        out_specs=(vmem, vmem),
        scratch_shapes=[
            pltpu.VMEM((3, BX + 4, 32, NZ), f32),
            pltpu.VMEM((3, BX, BY, NZ), f32),
            pltpu.VMEM((3, BX, BY, NZ), f32),
            pltpu.VMEM((NZ, NZ), f32),
            pltpu.VMEM((NZ, NZ), f32),
            pltpu.VMEM((LARGE, 512), bf16),
            pltpu.VMEM((2 * MID, 256), bf16),
            pltpu.VMEM((4 * NARROW, 128), bf16),
            pltpu.VMEM((3, BX, BY, NZ), f32),
            pltpu.VMEM((2, 160, NZ), f32),
            pltpu.VMEM((NZ, NZ), bf16),
            pltpu.VMEM((NZ, NZ), bf16),
            pltpu.VMEM((NZ, NZ), bf16),
            pltpu.VMEM((NZ, NZ), bf16),
            pltpu.VMEM((2, 3, 16, NZ), f32),
            pltpu.VMEM((2, 3, 16, NZ), f32),
            pltpu.VMEM((2, NZ // 2, 128), f32),
            pltpu.VMEM((NZ, 128), f32),
            pltpu.VMEM((NZ, 128), f32),
            pltpu.VMEM((2, NZ // 2, 128), f32),
            pltpu.VMEM((3, BX + 4, BY, NZ), f32),
            pltpu.VMEM((BX + 4, BY, NZ), f32),
            pltpu.VMEM((2, 3, 2, BY, NZ), f32),
            pltpu.VMEM((2, 3, 2, BY, NZ), f32),
            pltpu.VMEM((2, 3, 16, NZ), f32),
            pltpu.VMEM((2, 3, 16, NZ), f32),
            pltpu.VMEM((2, 128, NZ), f32),
            pltpu.VMEM((128, NZ), f32),
            pltpu.VMEM((2, 64, 128), f32),
            pltpu.SemaphoreType.DMA((3,)),
            pltpu.SemaphoreType.DMA((3,)),
            pltpu.SemaphoreType.DMA((10,)),
            pltpu.SemaphoreType.DMA((10,)),
            pltpu.SemaphoreType.DMA((12,)),
            pltpu.SemaphoreType.REGULAR,
        ],
        compiler_params=pltpu.CompilerParams(
            collective_id=0, has_side_effects=True, vmem_limit_bytes=52 * 1024 * 1024
        ),
    )(
        velocity_now, advecting, cotangent, small, vertical_modes, vertical_tilt, tables(),
    )
    return pl.pallas_call(
        write_out,
        out_shape=(field, field),
        in_specs=[vmem, vmem],
        out_specs=(hbm, hbm),
        scratch_shapes=[pltpu.SemaphoreType.DMA((2,))],
        compiler_params=pltpu.CompilerParams(vmem_limit_bytes=8 * 1024 * 1024),
    )(*results)


def solution(mesh):
    blocks = P(None, "gx", "gy", None)
    return jax.shard_map(
        per_device,
        mesh=mesh,
        in_specs=(blocks, blocks, blocks, P("gx", "gy"), P(), P(), P(), P()),
        out_specs=(blocks, blocks),
        check_vma=False,
    )
```

```python
import functools
import math

import jax
import jax.numpy as jnp
import ml_dtypes
import numpy as np
from jax import lax
from jax.experimental import pallas as pl
from jax.experimental.pallas import tpu as pltpu
from jax.sharding import PartitionSpec as P

MESH = pl.DeviceIdType.MESH
BX, BY = 8, 16
GX, GY = 8, 16
NX, NY, NZ = 64, 256, 512
DEVICES = GX * GY
OWNERS = DEVICES // 2
OWNED = NZ // OWNERS // 2
SLOTS = 64
LARGE, MID, NARROW = 256, 992, 752
f32, bf16 = jnp.float32, jnp.bfloat16


def fourier(n):
    place = np.arange(n)
    basis = np.zeros((n, n))
    freq = np.zeros(n)
    for column in range(n):
        k = (column + 1) // 2
        angle = 2.0 * math.pi * k * place / n
        if column == 0 or k == n // 2:
            basis[:, column] = np.cos(angle) / math.sqrt(n)
        else:
            basis[:, column] = (np.cos(angle) if column % 2 else np.sin(angle)) * math.sqrt(2.0 / n)
        freq[column] = 2.0 - 2.0 * math.cos(2.0 * math.pi * k / n)
    return basis, freq


def split_const(matrix, count=2):
    parts = []
    for _ in range(count):
        parts.append(matrix.astype(ml_dtypes.bfloat16))
        matrix = matrix - parts[-1].astype(np.float64)
    return parts


def tables():
    j, k = np.arange(BX), np.arange(BY)
    sin_x = math.sqrt(2.0 / BX) * np.sin(math.pi * np.outer(j, j) / BX)
    sin_y = math.sqrt(2.0 / BY) * np.sin(math.pi * np.outer(k, k) / BY)
    sin_x[0], sin_x[:, 0], sin_y[0], sin_y[:, 0] = 0.0, 0.0, 0.0, 0.0
    sine = np.kron(sin_x, sin_y)
    mu = (2.0 - 2.0 * np.cos(math.pi * j / BX))[:, None] + (2.0 - 2.0 * np.cos(math.pi * k / BY))
    near = np.zeros((SLOTS, BX * BY))
    own = np.zeros((SLOTS, BX * BY))
    for y in range(BY):
        own[y, y] = 1.0
        if y:
            near[y] = sine[1 * BY + y]
            near[16 + y] = sine[(BX - 1) * BY + y]
    for x in range(1, BX):
        own[32 + x, x * BY] = 1.0
        near[32 + x] = sine[x * BY + 1]
        near[40 + x] = sine[x * BY + BY - 1]
    to_slots = np.concatenate([near, own], 1)
    from_slots = np.concatenate([sine, own.T], 1)
    qx, lx = fourier(NX)
    qy, ly = fourier(NY)
    order = np.zeros((GY, 2, BX, BX, 2, GY))
    for g in range(GY):
        for kind in range(2):
            for x in range(BX):
                order[g, kind, x, x, kind, g] = 1.0
    order = order.reshape(256, 256)
    rows = np.zeros((2, OWNED, NX, 2, 2, GX, OWNED))
    for group in range(2):
        for mode in range(OWNED):
            for g in range(GX):
                for kind in range(2):
                    rows[group, mode, :, kind, group, g, mode] = qx[8 * (g + kind) % NX]
    rows = rows.reshape(512, 128)
    cols = qx.reshape(GX, BX, NX).transpose(2, 1, 0).reshape(NX, NX)
    wc = np.stack([qy[0::16], np.roll(qy[0::16], -1, axis=0)]).reshape(32, 256)
    lam_x = np.tile(lx, 2 * OWNED)

    def columns(values):
        out = np.zeros((values.size, 128), ml_dtypes.bfloat16)
        for n, part in enumerate(split_const(values.reshape(-1), 3)):
            out[:, n] = part
        return out

    def packed(matrices, lanes):
        parts = []
        for matrix in matrices:
            for part in split_const(np.ascontiguousarray(matrix)):
                parts.append(np.pad(part, ((0, 0), (0, lanes - part.shape[1]))))
        return np.concatenate(parts)

    exact = np.concatenate([order, order.T]).astype(ml_dtypes.bfloat16)
    lam_y = np.stack(split_const(ly, 3)).reshape(6, 128)
    large = packed([rows.T], 512)
    mid = np.concatenate([exact, packed([qy, qy.T, wc, to_slots, from_slots], 256)])
    narrow = np.concatenate([packed([sine, rows, near.T, wc.T, cols, cols.T], 128), columns(lam_x), columns(mu), lam_y])
    narrow = np.pad(narrow, ((0, 4 * NARROW - narrow.shape[0]), (0, 0)))
    mid = np.concatenate([mid[:MID], mid[MID:]], axis=1)
    narrow = np.concatenate([narrow[NARROW * i : NARROW * i + NARROW] for i in range(4)], axis=1)
    return jnp.asarray(np.concatenate([large, mid, narrow]))


def summed(parts):
    parts = parts.astype(f32)
    return parts[:, 0:1] + (parts[:, 1:2] + parts[:, 2:3])


def unpacked(ref, start, rows, lanes):
    return ref[start : start + rows, :lanes], ref[start + rows : start + 2 * rows, :lanes]


def halves(value):
    high = value.astype(bf16)
    low = (value - high.astype(f32)).astype(bf16)
    return high, low


def dot(a, b, nt=False):
    dims = (((1,), (1 if nt else 0,)), ((), ()))
    return lax.dot_general(a, b, dims, preferred_element_type=f32)


def regroup(blocks):
    blocks = list(blocks)
    lanes = 128 // len(blocks)
    group = lax.broadcasted_iota(jnp.int32, blocks[0].shape, 1) // lanes
    step = len(blocks) // 2
    while step:
        low = (group & step) == 0
        for i in range(len(blocks)):
            if not i & step:
                a, b = blocks[i], blocks[i + step]
                blocks[i] = jnp.where(low, a, pltpu.roll(b, lanes * step, 1))
                blocks[i + step] = jnp.where(low, pltpu.roll(a, 128 - lanes * step, 1), b)
        step //= 2
    return blocks


def regroup_wide(blocks):
    out = []
    for right in range(2):
        quads = [regroup([b[:, 128 * right : 128 * right + 128] for b in blocks[4 * n : 4 * n + 4]]) for n in range(2)]
        out.extend(jnp.concatenate([a, b], axis=1) for a, b in zip(*quads))
    return out


def dot3(a, b, nt=False):
    n = a[0].shape[0]
    both = dot(jnp.concatenate([a[0], a[1]], axis=0), b[0], nt)
    return both[:n] + (dot(a[0], b[1], nt) + both[n:])


def wide(column, lanes):
    return jnp.concatenate([column] * (lanes // 128), axis=1)


TAPS = ((-2, 1.0, 1.0), (-1, -8.0, -4.0), (0, 0.0, 6.0), (1, 8.0, -4.0), (2, -1.0, 1.0))


def weights(speed):
    size = jnp.abs(speed)
    out = {}
    for offset, central, hyper in TAPS:
        out[offset] = hyper * size + central * speed if central else hyper * size
    return out


def moved(value, offset, axis):
    n = value.shape[axis]
    if axis == 1:
        rolled = pltpu.roll(value, (-offset) % n, 1)
    else:
        rolled = jnp.roll(value, -offset, 0)
    place = lax.broadcasted_iota(jnp.int32, value.shape, axis)
    keep = place < n - offset if offset > 0 else place >= -offset
    return jnp.where(keep, rolled, 0.0)


def kernel(
    vel_h, adv_h, cot_h, small, vm_h, vt_h, tables_h,
    next_ref, adj_ref,
    vb, adv, cot, vm_ref, vt_ref, large, mid, narrow,
    sv, lhs, vh, vl, th, tl, ys, yr, sb, rbuf, ob, rb, gp, sxp, cxs, cxr, cys, cyr,
    p1_ref, ie_ref, cs,
    a_send, a_recv, h_send, h_recv, l_sem, all_sem,
):
    gx, gy = lax.axis_index("gx"), lax.axis_index("gy")
    me = gx * GY + gy
    left_x, right_x = lax.rem(gx + GX - 1, GX), lax.rem(gx + 1, GX)
    left_y, right_y = lax.rem(gy + GY - 1, GY), lax.rem(gy + 1, GY)

    parity, half_y = lax.rem(gy, 2), lax.div(gy, 2)
    owner = gx * 8 + half_y
    barrier = pltpu.get_barrier_semaphore()
    for i in range(1, GX):
        pl.semaphore_signal(barrier, inc=1, device_id=(lax.rem(gx + i, GX), gy), device_id_type=MESH)
    for i in range(1, GY):
        pl.semaphore_signal(barrier, inc=1, device_id=(gx, lax.rem(gy + i, GY)), device_id_type=MESH)

    loads = [
        pltpu.make_async_copy(source, target, l_sem.at[n])
        for n, (source, target) in enumerate(
            (
                (vel_h, vb.at[:, pl.ds(2, BX), pl.ds(8, BY)]),
                (vm_h, vm_ref),
                (vt_h, vt_ref),
                (cot_h, cot),
                (adv_h, adv),
                (tables_h.at[pl.ds(0, LARGE)], large),
            )
            + tuple(
                (tables_h.at[pl.ds(LARGE + MID, NARROW), pl.ds(128 * i, 128)], narrow.at[pl.ds(NARROW * i, NARROW)])
                for i in range(4)
            )
            + tuple(
                (tables_h.at[pl.ds(LARGE, MID), pl.ds(256 * i, 256)], mid.at[pl.ds(MID * i, MID)])
                for i in range(2)
            )
        )
    ]
    for n in (0, 3, 1, 2, 6, 7, 8, 9, 10, 11, 4, 5):
        loads[n].start()
    pl.semaphore_wait(barrier, GX + GY - 2)

    def remote(src, dst, n, x, y):
        return pltpu.make_async_remote_copy(
            src_ref=src, dst_ref=dst, send_sem=h_send.at[n], recv_sem=h_recv.at[n],
            device_id=(x, y), device_id_type=MESH,
        )

    halo = [
        remote(vel_h.at[:, pl.ds(0, 2)], vb.at[:, pl.ds(BX + 2, 2), pl.ds(8, BY)], 0, left_x, gy),
        remote(vel_h.at[:, pl.ds(BX - 2, 2)], vb.at[:, pl.ds(0, 2), pl.ds(8, BY)], 1, right_x, gy),
        remote(ys.at[0], yr.at[1], 2, gx, left_y),
        remote(ys.at[1], yr.at[0], 3, gx, right_y),
    ]

    for i in range(1, GY):
        pl.semaphore_signal(all_sem, inc=1, device_id=(gx, lax.rem(gy + i, GY)), device_id_type=MESH)

    loads[0].wait()

    for c in range(3):
        for x in range(BX):
            ys[0, c, 2 * x : 2 * x + 2, :] = vb[c, x + 2, 8:10, :]
            ys[1, c, 2 * x : 2 * x + 2, :] = vb[c, x + 2, 6 + BY : 8 + BY, :]
    halo[2].start()
    halo[3].start()

    loads[1].wait()
    loads[2].wait()
    for full, high, low in ((vm_ref, vh, vl), (vt_ref, th, tl)):
        for i in range(0, NZ, 64):
            h, l = halves(full[i : i + 64, :])
            high[i : i + 64, :] = h
            low[i : i + 64, :] = l
    for n in range(6, 10):
        loads[n].wait()
    rate_row = jnp.concatenate([small[n : n + 1, :] for n in range(4)], axis=1)
    ie_ref[...] = 1.0 / (summed(narrow[2816:2944, :]) + rate_row)

    factor = small[4:5, 0:1]
    scale = factor * f32(-1.0 / 12.0)

    levels = lax.broadcasted_iota(jnp.int32, (BY, NZ), 1).astype(f32)
    diagonal = lax.broadcasted_iota(jnp.int32, (BY, BY), 0) == lax.broadcasted_iota(
        jnp.int32, (BY, BY), 1
    )

    def fluid_at(x):
        row = small[pl.ds(8 + x, 1), 0:BY]
        column = jnp.sum(jnp.where(diagonal, row, 0.0), axis=1, keepdims=True)
        return (levels >= column).astype(f32)

    def left_sides(group, field):
        for x in range(BX):
            f0 = field[0, x]
            if x:
                f0 = f0 - field[0, x - 1]
            f1 = field[1, x]
            lhs[group, BY * x : BY * x + BY, :] = f0 + (f1 - moved(f1, -1, 0))
            lhs[group, 144 + x : 145 + x, :] = -field[1, x, BY - 1 : BY, :]
        lhs[group, 128:144, :] = -field[0, BX - 1]
        lhs[group, 152:160, :] = jnp.zeros((8, NZ), f32)

    def forward(group, field):
        left_sides(group, field)
        wide_rows = dot3(halves(lhs[group]), (vh[...], vl[...]))
        tilted = dot3(halves(field[2].reshape(BX * BY, NZ)), (th[...], tl[...]))
        d = wide_rows[:128] + tilted
        d_parts = halves(d)
        p1 = dot3(unpacked(narrow, 0, 128, 128), d_parts)
        p1_ref[group] = p1
        w = halves(p1 * ie_ref[...])
        both = (
            jnp.concatenate([w[0], d_parts[0]], axis=0),
            jnp.concatenate([w[1], d_parts[1]], axis=0),
        )
        s = dot3(unpacked(mid, 1600, 64, 256), both)
        some, few = jnp.zeros((16, NZ), f32), jnp.zeros((8, NZ), f32)
        s = s + jnp.concatenate([some, wide_rows[128:144], few, wide_rows[144:152], some], axis=0)
        s = jnp.concatenate([s[:, : NZ // 2], s[:, NZ // 2 :]], axis=0)
        for i in range(2):
            sb[group, 128 * i : 128 * i + 128, :] = s[:, 128 * i : 128 * i + 128].T

    def chunk(n):
        return pl.ds(n * OWNED, OWNED)

    place = gy * GX + gx

    def to_owners(group):
        def copy_to(dx, dy):
            tx, ty = lax.rem(gx + dx, GX), lax.rem(half_y + dy, 8)
            return pltpu.make_async_remote_copy(
                src_ref=sb.at[group, chunk(tx * 8 + ty)], dst_ref=rbuf.at[chunk(place)],
                send_sem=a_send.at[group], recv_sem=a_recv.at[0],
                device_id=(tx, ty * 2 + group), device_id_type=MESH,
            )

        @pl.when(parity != group)
        def _():
            copy_to(0, 0).start()

        @pl.when(parity == group)
        def _():
            pltpu.make_async_copy(sb.at[group, chunk(owner)], rbuf.at[chunk(place)], a_recv.at[0]).start()

        def start(dx, carry):
            for dy in range(8):
                copy_to(dx, dy).start()
            return carry

        for dy in range(1, 8):
            copy_to(0, dy).start()
        lax.fori_loop(1, GX, start, 0)

    def span(ref, chunks, send, recv):
        rows = ref.at[pl.ds(0, chunks * OWNED)]
        return pltpu.make_async_remote_copy(
            src_ref=rows, dst_ref=rows, send_sem=a_send.at[send], recv_sem=a_recv.at[recv],
            device_id=(right_x, gy), device_id_type=MESH,
        )

    loads[3].wait()
    loads[10].wait()
    loads[11].wait()
    forward(1, cot)
    pl.semaphore_wait(all_sem, GY - 1)
    to_owners(1)
    halo[0].start()
    halo[1].start()

    loads[4].wait()
    def own():
        loads[5].wait()
        span(rbuf, DEVICES, 0, 0).wait_recv()
        sides = [
            regroup([rbuf[32 * (8 * half + i) : 32 * (8 * half + i) + 32, :] for i in range(8)])
            for half in range(2)
        ]
        rows = [jnp.concatenate([sides[0][j], sides[1][j]], axis=1) for j in range(8)]
        along = dot3(halves(jnp.concatenate([rows[0], rows[4], rows[1], rows[5]], axis=0)), unpacked(mid, 512, 256, 256))
        columns = halves(jnp.concatenate([rows[2], rows[6]], axis=0))
        columns = dot(columns[0], mid[0:256, :]) + dot(columns[1], mid[0:256, :])
        for n in range(2):
            cs[n] = columns[:, 128 * n : 128 * n + 128]
        picked = [
            jnp.concatenate([cs[n, pl.ds(32 * half + m, GX, stride=OWNED), :] for n in range(2)], axis=1)
            for half in range(2)
            for m in range(OWNED)
        ]
        columns = halves(jnp.concatenate(regroup_wide(picked), axis=0))
        inner = dot3(unpacked(narrow, 2048, 64, 64), columns)
        inner = halves(jnp.concatenate([inner[:, 32 * n : 32 * n + 32] for n in range(8)], axis=0))
        along = halves(along)
        row_table, edge_table = unpacked(narrow, 256, 512, 128), unpacked(mid, 1536, 32, 256)
        left = [jnp.concatenate([row_table[i], inner[i]], axis=1) for i in range(2)]
        right = [jnp.concatenate([along[i], edge_table[i]], axis=0) for i in range(2)]
        hat = dot3(left, right)
        row = lax.broadcasted_iota(jnp.int32, (512, 128), 0)
        row_mode = lax.div(row, NX)
        rate = jnp.zeros((512, 128), f32)
        lane = lax.broadcasted_iota(jnp.int32, (1, 128), 1)
        first_lane = lax.rem(owner, 128 // OWNED) * OWNED
        for half in range(2):
            rates = small[pl.ds(2 * half + lax.div(owner, 128 // OWNED), 1), :]
            for m in range(OWNED):
                one = jnp.sum(jnp.where(lane == first_lane + m, rates, 0.0), axis=1, keepdims=True)
                rate = jnp.where(row_mode == OWNED * half + m, one, rate)
        lam_y = narrow[2944:2960, :].astype(f32)
        lam_y = [lam_y[n : n + 1] + (lam_y[n + 2 : n + 3] + lam_y[n + 4 : n + 5]) for n in range(2)]
        lam_y = jnp.concatenate(lam_y, axis=1)
        hat = halves(hat / (wide(rate + summed(narrow[2304:2816, :]), 256) + lam_y))
        along = dot3(halves(dot3(unpacked(large, 0, 128, 512), hat)), unpacked(mid, 1024, 256, 256))
        inner = dot3(hat, unpacked(narrow, 1536, 256, 32))
        inner = halves(jnp.concatenate([inner[NX * n : NX * n + NX] for n in range(8)], axis=1))
        columns = dot3(unpacked(narrow, 2176, 64, 64), inner)
        picked = regroup_wide([columns[8 * x : 8 * x + 8] for x in range(BX)])
        for half in range(2):
            for m in range(OWNED):
                for n in range(2):
                    block = picked[OWNED * half + m][:, 128 * n : 128 * n + 128]
                    cs[n, pl.ds(32 * half + m, GX, stride=OWNED), :] = block
        columns = halves(jnp.concatenate([cs[0], cs[1]], axis=1))
        columns = dot(columns[0], mid[256:512, :]) + dot(columns[1], mid[256:512, :])
        nothing = jnp.zeros((32, 256), f32)
        rows = [along[0:32], along[64:96], columns[0:32], nothing, along[32:64], along[96:128], columns[32:64], nothing]
        for half in range(2):
            for i, block in enumerate(regroup([r[:, 128 * half : 128 * half + 128] for r in rows])):
                ob[32 * (8 * half + i) : 32 * (8 * half + i) + 32, :] = block

        pltpu.make_async_copy(ob.at[chunk(place)], rb.at[parity, chunk(owner)], a_recv.at[1 + parity]).start()

        def answer(dx, dy):
            tx, ty = lax.rem(gx + dx, GX), lax.rem(gy + dy, GY)
            pltpu.make_async_remote_copy(
                src_ref=ob.at[chunk(ty * GX + tx)], dst_ref=rb.at[parity, chunk(owner)],
                send_sem=a_send.at[2], recv_sem=a_recv.at[1 + parity],
                device_id=(tx, ty), device_id_type=MESH,
            ).start()

        def answers(dx, carry):
            for dy in range(GY):
                answer(dx, dy)
            return carry

        for dy in range(1, GY):
            answer(0, dy)
        lax.fori_loop(1, GX, answers, 0)

    pl.when(parity == 1)(own)
    halo[2].wait()
    halo[3].wait()
    for c in range(3):
        for x in range(BX):
            vb[c, x + 2, 6:8, :] = yr[0, c, 2 * x : 2 * x + 2, :]
            vb[c, x + 2, 8 + BY : 10 + BY, :] = yr[1, c, 2 * x : 2 * x + 2, :]

    def section_row(x, carry):
        fluid = fluid_at(x)
        kx, ky, kz = weights(adv[0, x]), weights(adv[1, x]), weights(adv[2, x])
        for c in range(3):
            center = vb[c, x + 2, 8 : 8 + BY, :]
            total = center * (kx[0] + ky[0] + kz[0])
            for offset in (-2, -1, 1, 2):
                total = total + kx[offset] * vb[c, x + 2 + offset, 8 : 8 + BY, :]
                total = total + ky[offset] * vb[c, x + 2, 8 + offset : 8 + BY + offset, :]
                total = total + kz[offset] * moved(center, offset, 1)
            sv[c, x] = fluid * (center + scale * total)
        return carry

    lax.fori_loop(2, BX - 2, section_row, 0)
    halo[0].wait()
    halo[1].wait()
    lax.fori_loop(0, 2, section_row, 0)
    lax.fori_loop(BX - 2, BX, section_row, 0)
    forward(0, sv)

    to_owners(0)

    def backward(group):
        span(rb.at[group], OWNERS, 0, 1 + group).wait_recv()
        u = jnp.concatenate([rb[group, 0:128, :].T, rb[group, 128:256, :].T], axis=1)
        u = jnp.concatenate([u[0:SLOTS], u[SLOTS:]], axis=1)
        u_parts = halves(u)
        inside = (p1_ref[group] + dot3(unpacked(narrow, 1280, 128, 64), u_parts)) * ie_ref[...]
        in_parts = halves(inside)
        both = (
            jnp.concatenate([in_parts[0], u_parts[0]], axis=0),
            jnp.concatenate([in_parts[1], u_parts[1]], axis=0),
        )
        phi = dot3(unpacked(mid, 1728, 128, 192), both)
        ext = jnp.concatenate([phi, u[16:32], u[40:48], jnp.zeros((8, NZ), f32)], axis=0)
        lhs[group] = dot3(halves(ext), (vh[...], vl[...]), nt=True)
        return halves(phi)

    def tilt(phi):
        return dot3(phi, (th[...], tl[...]), nt=True)

    def corrections(group, x):
        here = lhs[group, BY * x : BY * x + BY, :]
        after = lhs[group, BY * x + BY : BY * x + 2 * BY, :]
        last = lax.broadcasted_iota(jnp.int32, (BY, NZ), 0) == BY - 1
        side = jnp.where(last, lhs[group, 144 + x : 145 + x, :], jnp.roll(here, -1, 0))
        return here - after, here - side

    phi = backward(1)

    def gradient_row(x):
        fluid = fluid_at(x)
        c0, c1 = corrections(1, x)
        gp[0, x + 2] = fluid * (cot[0, x] - c0)
        gp[1, x + 2] = fluid * (cot[1, x] - c1)
        sxp[x + 2] = adv[0, x]

    def gradient_row_z(x):
        gp[2, x + 2] = fluid_at(x) * (cot[2, x] - tilted[BY * x : BY * x + BY])

    for x in (0, 1, BX - 2, BX - 1):
        gradient_row(x)

    k0, k1 = weights(adv[0, 0]), weights(adv[0, 1])
    k6, k7 = weights(adv[0, BX - 2]), weights(adv[0, BX - 1])
    edges = [
        remote(cxs.at[0, pl.ds(0, 2)], cxr.at[1, pl.ds(0, 2)], 4, left_x, gy),
        remote(cxs.at[1, pl.ds(0, 2)], cxr.at[0, pl.ds(0, 2)], 5, right_x, gy),
        remote(cys.at[0], cyr.at[1], 6, gx, left_y),
        remote(cys.at[1], cyr.at[0], 7, gx, right_y),
        remote(cxs.at[0, pl.ds(2, 1)], cxr.at[1, pl.ds(2, 1)], 8, left_x, gy),
        remote(cxs.at[1, pl.ds(2, 1)], cxr.at[0, pl.ds(2, 1)], 9, right_x, gy),
    ]

    def contributions_x(c):
        g0, g1, g6, g7 = gp[c, 2], gp[c, 3], gp[c, BX], gp[c, BX + 1]
        cxs[0, c, 0] = k0[-2] * g0
        cxs[0, c, 1] = k0[-1] * g0 + k1[-2] * g1
        cxs[1, c, 0] = k7[1] * g7 + k6[2] * g6
        cxs[1, c, 1] = k7[2] * g7

    contributions_x(0)
    contributions_x(1)
    edges[0].start()
    edges[1].start()
    tilted = tilt(phi)
    for x in (0, 1, BX - 2, BX - 1):
        gradient_row_z(x)
    contributions_x(2)
    edges[4].start()
    edges[5].start()
    for x in range(2, BX - 2):
        gradient_row(x)
        gradient_row_z(x)
    for x in range(BX):
        k = weights(adv[1, x])
        for c in range(3):
            g = gp[c, x + 2]
            one, two = k[-1] * g, k[-2] * g
            cys[0, c, 2 * x : 2 * x + 1, :] = two[0:1]
            cys[0, c, 2 * x + 1 : 2 * x + 2, :] = one[0:1] + two[1:2]
            one, two = k[1] * g, k[2] * g
            cys[1, c, 2 * x : 2 * x + 1, :] = one[BY - 1 : BY] + two[BY - 2 : BY - 1]
            cys[1, c, 2 * x + 1 : 2 * x + 2, :] = two[BY - 1 : BY]
    edges[2].start()
    edges[3].start()
    pl.when(parity == 0)(own)
    nothing = jnp.zeros((2, BY, NZ), f32)
    for c in range(3):
        gp[c, 0:2] = nothing
        gp[c, BX + 2 : BX + 4] = nothing
    sxp[0:2] = nothing
    sxp[BX + 2 : BX + 4] = nothing

    def adjoint_row(x, carry):
        kx = {}
        for offset in (-2, -1, 0, 1, 2):
            kx[offset] = weights(sxp[x + 2 - offset])[offset]
        ky, kz = weights(adv[1, x]), weights(adv[2, x])
        for c in range(3):
            center = gp[c, x + 2]
            total = center * (kx[0] + ky[0] + kz[0])
            for offset in (-2, -1, 1, 2):
                total = total + kx[offset] * gp[c, x + 2 - offset]
                total = total + moved(ky[offset] * center, -offset, 0)
                total = total + moved(kz[offset] * center, -offset, 1)
            adj_ref[c, x] = center + scale * total
        return carry

    lax.fori_loop(0, BX, adjoint_row, 0)

    tilted = tilt(backward(0))
    for x in range(BX):
        c0, c1 = corrections(0, x)
        next_ref[0, x] = sv[0, x] - c0
        next_ref[1, x] = sv[1, x] - c1
        next_ref[2, x] = sv[2, x] - tilted[BY * x : BY * x + BY]

    for copy in edges:
        copy.wait()
    for c in range(3):
        for n in range(2):
            adj_ref[c, n] += scale * cxr[0, c, n]
            adj_ref[c, BX - 2 + n] += scale * cxr[1, c, n]
        for x in range(BX):
            adj_ref[c, x, 0:2, :] += scale * cyr[0, c, 2 * x : 2 * x + 2, :]
            adj_ref[c, x, BY - 2 : BY, :] += scale * cyr[1, c, 2 * x : 2 * x + 2, :]

    span(rbuf, DEVICES - 1, 2, 0).wait_send()
    for group in range(2):

        @pl.when(parity != group)
        def _():
            span(rbuf, OWNERS, group, 0).wait_send()

        @pl.when(parity == group)
        def _():
            span(rbuf, OWNERS - 1, group, 0).wait_send()


def write_out(next_ref, adj_ref, next_out, adj_out, sems):
    copies = [
        pltpu.make_async_copy(next_ref, next_out, sems.at[0]),
        pltpu.make_async_copy(adj_ref, adj_out, sems.at[1]),
    ]
    for copy in copies:
        copy.start()
    for copy in copies:
        copy.wait()


def section_factor(section_index):
    section = lax.rem(section_index[0], 3)
    step = lax.div(section_index[0], 3).astype(f32)
    size = f32(0.2) + f32(0.2) * step / f32(63.0)
    return size * jnp.where(section == 0, f32(1.0 / 3.0), jnp.where(section == 1, f32(0.5), f32(1.0)))


def per_device(
    velocity_now, advecting, cotangent, building_height, section_index,
    vertical_modes, vertical_tilt, mode_rates,
):
    small = jnp.concatenate(
        [
            mode_rates.reshape(4, 128),
            jnp.broadcast_to(section_factor(section_index), (4, 128)),
            jnp.pad(building_height, ((0, 0), (0, 128 - BY))).astype(f32),
        ]
    )
    vmem = pl.BlockSpec(memory_space=pltpu.VMEM)
    hbm = pl.BlockSpec(memory_space=pltpu.HBM)
    field = jax.ShapeDtypeStruct((3, BX, BY, NZ), f32)
    results = pl.pallas_call(
        kernel,
        out_shape=(field, field),
        in_specs=[hbm, hbm, hbm, vmem, hbm, hbm, hbm],
        out_specs=(vmem, vmem),
        scratch_shapes=[
            pltpu.VMEM((3, BX + 4, 32, NZ), f32),
            pltpu.VMEM((3, BX, BY, NZ), f32),
            pltpu.VMEM((3, BX, BY, NZ), f32),
            pltpu.VMEM((NZ, NZ), f32),
            pltpu.VMEM((NZ, NZ), f32),
            pltpu.VMEM((LARGE, 512), bf16),
            pltpu.VMEM((2 * MID, 256), bf16),
            pltpu.VMEM((4 * NARROW, 128), bf16),
            pltpu.VMEM((3, BX, BY, NZ), f32),
            pltpu.VMEM((2, 160, NZ), f32),
            pltpu.VMEM((NZ, NZ), bf16),
            pltpu.VMEM((NZ, NZ), bf16),
            pltpu.VMEM((NZ, NZ), bf16),
            pltpu.VMEM((NZ, NZ), bf16),
            pltpu.VMEM((2, 3, 16, NZ), f32),
            pltpu.VMEM((2, 3, 16, NZ), f32),
            pltpu.VMEM((2, NZ // 2, 128), f32),
            pltpu.VMEM((NZ, 128), f32),
            pltpu.VMEM((NZ, 128), f32),
            pltpu.VMEM((2, NZ // 2, 128), f32),
            pltpu.VMEM((3, BX + 4, BY, NZ), f32),
            pltpu.VMEM((BX + 4, BY, NZ), f32),
            pltpu.VMEM((2, 3, 2, BY, NZ), f32),
            pltpu.VMEM((2, 3, 2, BY, NZ), f32),
            pltpu.VMEM((2, 3, 16, NZ), f32),
            pltpu.VMEM((2, 3, 16, NZ), f32),
            pltpu.VMEM((2, 128, NZ), f32),
            pltpu.VMEM((128, NZ), f32),
            pltpu.VMEM((2, 64, 128), f32),
            pltpu.SemaphoreType.DMA((3,)),
            pltpu.SemaphoreType.DMA((3,)),
            pltpu.SemaphoreType.DMA((10,)),
            pltpu.SemaphoreType.DMA((10,)),
            pltpu.SemaphoreType.DMA((12,)),
            pltpu.SemaphoreType.REGULAR,
        ],
        compiler_params=pltpu.CompilerParams(
            collective_id=0, has_side_effects=True, vmem_limit_bytes=52 * 1024 * 1024
        ),
    )(
        velocity_now, advecting, cotangent, small, vertical_modes, vertical_tilt, tables(),
    )
    return pl.pallas_call(
        write_out,
        out_shape=(field, field),
        in_specs=[vmem, vmem],
        out_specs=(hbm, hbm),
        scratch_shapes=[pltpu.SemaphoreType.DMA((2,))],
        compiler_params=pltpu.CompilerParams(vmem_limit_bytes=8 * 1024 * 1024),
    )(*results)


def solution(mesh):
    blocks = P(None, "gx", "gy", None)
    return jax.shard_map(
        per_device,
        mesh=mesh,
        in_specs=(blocks, blocks, blocks, P("gx", "gy"), P(), P(), P(), P()),
        out_specs=(blocks, blocks),
        check_vma=False,
    )
```
